32 devices in a mesh: dp: 8 (over z, y), expert: 4 (over x, core).
Axes of the slice: x: 2, y: 2, z: 4, core: 2. Of those that a mesh axis runs over, the one named last changes fastest.
Arguments:
- tokens: bfloat16 [4096, 2048], P(('dp', 'expert')), may hold values from -6 to 6
- expert_ids: int32 [4096, 2], P(('dp', 'expert')), may hold values from 0 to 3, all different within a row; in each aligned block of 128 rows (0 to 127, 128 to 255, ...) at most 66 rows name the same one
- gate_probs: bfloat16 [4096, 2], P(('dp', 'expert')), may hold values from 0.099609375 to 1
- w_gate: bfloat16 [4, 2048, 768], P('expert'), may hold values from -0.125 to 0.125
- w_up: bfloat16 [4, 2048, 768], P('expert'), may hold values from -0.125 to 0.125
- w_down: bfloat16 [4, 768, 2048], P('expert'), may hold values from -0.21875 to 0.21875
- teacher_queries: bfloat16 [4, 8, 2048], P('expert', 'dp'), may hold values from -6 to 6
- teacher_passages: bfloat16 [4, 16, 2048], P('expert', 'dp'), may hold values from -6 to 6
- positives: int32 [4, 8], P('expert', 'dp'), may hold values from 0 to 15
Outputs:
- moe_out: bfloat16 [4096, 2048], P(('dp', 'expert'))
- token_grad: bfloat16 [4096, 2048], P(('dp', 'expert'))
- gate_grad: float32 [4096, 2], P(('dp', 'expert'))
- query_loss: float32 [4, 8], P('expert', 'dp')
The draws below stay inside these ranges and needn't reach their ends.
Inputs may be any that keep to these rules, and one draw needn't show every extreme that they name: `expert_ids`: each token names 2 different experts of its group; among the 128 tokens of one device no expert is named more than 66 times, a bound that some block reaches.
All inputs are finite; a program needn't handle non-finite values.
Results may differ from the reference program's by a relative error of at most 0.015.
Values may be sent and summed in bfloat16 or wider, within the bound.
A program may use at most 64 MiB of HBM per device.

```python
import math
import jax
import jax.numpy as jnp
import numpy as np
from jax import lax

D = 2048
FF = 768
TOP = 2
Q_DEV = 1
QLEN = 32
PLEN = 48
EXPERTS = 4
PASS_DEV = 2
TOK_DEV = 128
CAP = 66
TOKENS = 4096
QROWS = 8
PROWS = 16
BATCHES = 4
N_DP = 8
N_EXPERT = 4


def plant(result, stream_key, least, largest):
    place = [jax.random.randint(jax.random.fold_in(stream_key, axis), (), 0, length) for axis, length in enumerate(result.shape)]
    widest = result.shape.index(max(result.shape))
    next_to = place[:widest] + [(place[widest] + 1) % result.shape[widest]] + place[widest + 1:]
    return result.at[tuple(place)].set(least).at[tuple(next_to)].set(largest)


def block_levels(own_key, extent, split, least, top_value):
    level, own = 1.0, jax.random.fold_in(own_key, 6)
    for axis_at, shards_of in split:
        steps = jnp.exp(jax.random.uniform(jax.random.fold_in(own, axis_at), (shards_of,), jnp.float32, least / len(split), top_value / len(split)))
        level = level * jnp.repeat(steps, extent[axis_at] // shards_of).reshape([-1 if axis == axis_at else 1 for axis in range(len(extent))])
    return level


def routed_block(rng, own, number, rows, amount, top, limit, lean):
    order = jax.random.permutation(rng, amount)
    packed, common = shares(amount, rows * top, limit, lean, True), shares(amount, rows * top, limit, lean, False)
    places = jnp.arange(amount)

    def named(sizes, rotation):
        used = int((sizes > 0).sum())
        fixed = max(1, used // 4)
        moved = fixed + (places - fixed + rotation * (used - fixed)) % max(1, amount - fixed)
        return jnp.zeros((amount,), jnp.int32).at[order[jnp.where(places < fixed, places, moved)]].set(jnp.asarray(sizes, jnp.int32))

    sizes = jnp.where(number % 4 == 0, named(packed, number // 4), named(common, number - number // 4 - 1))
    mixed = jax.random.permutation(jax.random.fold_in(own, 3), amount)
    giver, sink = mixed[0:amount // 2 * 2:2], mixed[1:amount // 2 * 2:2]
    slack = jnp.minimum(sizes[giver] - 1, limit - sizes[sink]) // 2
    slack = jnp.where((giver == order[0]) | (sink == order[0]) | (sizes[sink] == 0), 0, jnp.maximum(slack, 0))
    moved = jax.random.randint(jax.random.fold_in(own, 4), (amount // 2,), 0, 1 << 20) % (slack + 1)
    sizes = sizes.at[giver].add(-moved).at[sink].add(moved)
    members = jnp.searchsorted(jnp.cumsum(sizes), jnp.arange(rows * top), side="right").astype(jnp.int32)
    listing = members.reshape(top, rows).T
    listing = listing[jax.random.permutation(jax.random.fold_in(own, 1), rows)]
    rotation = jax.random.randint(jax.random.fold_in(own, 2), (rows, 1), 0, top)
    return jnp.take_along_axis(listing, (jnp.arange(top)[None, :] + rotation) % top, axis=1)


def shares(amount, total, bound, slope, full):
    weights = [(1 << 20) // math.isqrt(rank ** slope) + 1 for rank in range(1, amount + 1)]
    largest = bound if full else min(bound, max(-(-total // amount), total * weights[0] // sum(weights)))
    least = 1 if total - largest >= amount - 1 else 0
    counts, spare = [largest] + [least] * (amount - 1), total - largest - least * (amount - 1)
    while spare > 0:
        candidates = [i for i in range(1, amount) if counts[i] < largest] or [i for i in range(1, amount) if counts[i] < bound]
        whole, remaining = sum([weights[i] for i in candidates]), spare
        for i in candidates:
            addition = min(bound - counts[i], max(1, remaining * weights[i] // whole), spare)
            counts[i] = counts[i] + addition
            spare = spare - addition
    return np.array(counts)


def normal_values(rng, dims, spread, most, split=(), held_as=jnp.bfloat16):
    array = jax.random.normal(rng, dims, jnp.float32) * spread
    if len(split) > 0:
        array = block_levels(rng, dims, split, -0.22, 0.18) * array
    return jnp.clip(array, min=-most, max=most).astype(held_as)


def setup_inputs(seed: int = 0) -> dict:
    seeds = jax.random.split(jax.random.key(seed), 10)
    tokens = normal_values(seeds[0], (TOKENS, D), 1.0, 6.0, ((0, 32),))
    expert_ids_keys = jax.random.split(jax.random.fold_in(seeds[1], 1), TOKENS // TOK_DEV)
    expert_ids_turns = jax.random.permutation(jax.random.fold_in(seeds[1], 3), TOKENS // TOK_DEV)
    expert_ids = jax.vmap(lambda own, number: routed_block(jax.random.fold_in(seeds[1], 2), own, number, TOK_DEV, EXPERTS, TOP, CAP, 2))(expert_ids_keys, expert_ids_turns).reshape((TOKENS, TOP))
    gate_probs = jnp.clip(jnp.exp(math.log(1.0) - 2.306499 * jax.random.uniform(seeds[2], (TOKENS, TOP), jnp.float32) ** block_levels(seeds[2], (TOKENS, TOP), ((0, 32),), -0.2, 0.2)), 0.099609375, 1.0).astype(jnp.bfloat16)
    w_gate = normal_values(seeds[3], (EXPERTS, D, FF), D ** -0.5, 0.125, ((0, 4),))
    w_up = normal_values(seeds[4], (EXPERTS, D, FF), D ** -0.5, 0.125, ((0, 4),))
    w_down = normal_values(seeds[5], (EXPERTS, FF, D), FF ** -0.5, 0.21875, ((0, 4),))
    teacher_queries = normal_values(seeds[6], (BATCHES, QROWS, D), 1.0, 6.0, ((0, 4), (1, 8)))
    teacher_passages = normal_values(seeds[7], (BATCHES, PROWS, D), 1.0, 6.0, ((0, 4), (1, 8)))
    positives = plant(jax.random.randint(seeds[8], (BATCHES, QROWS), 0, PROWS), jax.random.fold_in(seeds[8], 1), 0, PROWS - 1).astype(jnp.int32)
    return dict(tokens=tokens, expert_ids=expert_ids, gate_probs=gate_probs, w_gate=w_gate, w_up=w_up, w_down=w_down, teacher_queries=teacher_queries, teacher_passages=teacher_passages, positives=positives)


student_scale = 50.0
teacher_scale = 80.0
loss_scale = 64.0
norm_eps = 1e-06
highest = lax.Precision.HIGHEST

def silu_slope(pre_gate):
    sigmoid = jax.nn.sigmoid(pre_gate)
    return sigmoid * (1.0 + pre_gate * (1.0 - sigmoid))

def expert_forward(expert_args):
    routed, gate_mat, up_mat, down_mat = expert_args
    routed_f = routed.astype(jnp.float32)
    pre_gate = jnp.dot(routed_f, gate_mat, precision=highest)
    pre_up = jnp.dot(routed_f, up_mat, precision=highest)
    hidden = (jax.nn.silu(pre_gate) * pre_up).astype(jnp.bfloat16)
    return jnp.dot(hidden.astype(jnp.float32), down_mat, precision=highest).astype(jnp.bfloat16)

def expert_apply(expert_args):
    routed, routed_grad, gate_mat, up_mat, down_mat = expert_args
    routed_f = routed.astype(jnp.float32)
    grad_f = routed_grad.astype(jnp.float32)
    pre_gate = jnp.dot(routed_f, gate_mat, precision=highest)
    pre_up = jnp.dot(routed_f, up_mat, precision=highest)
    activation = jax.nn.silu(pre_gate)
    hidden = (activation * pre_up).astype(jnp.bfloat16)
    expert_out = jnp.dot(hidden.astype(jnp.float32), down_mat, precision=highest).astype(jnp.bfloat16)
    hidden_grad = jnp.dot(grad_f, down_mat.T, precision=highest)
    gate_part = (hidden_grad * pre_up * silu_slope(pre_gate)).astype(jnp.bfloat16)
    up_part = (hidden_grad * activation).astype(jnp.bfloat16)
    row_grad = jnp.dot(gate_part.astype(jnp.float32), gate_mat.T, precision=highest)
    row_grad = row_grad + jnp.dot(up_part.astype(jnp.float32), up_mat.T, precision=highest)
    return (expert_out, row_grad.astype(jnp.bfloat16))

def slot_numbers(group_ids):
    flat_ids = group_ids.reshape(-1).astype(jnp.int32)
    per_source = TOK_DEV * TOP
    expert_hits = (flat_ids[:, None] == jnp.arange(EXPERTS, dtype=jnp.int32)[None, :]).astype(jnp.int32)
    blocks = expert_hits.reshape(N_EXPERT, per_source, EXPERTS)
    earlier = (jnp.cumsum(blocks, axis=1) - blocks).reshape(-1, EXPERTS)
    slot_rank = lax.optimization_barrier(jnp.sum(earlier * expert_hits, axis=1))
    source = jnp.arange(flat_ids.shape[0], dtype=jnp.int32) // per_source
    return (flat_ids * (N_EXPERT * CAP) + source * CAP + slot_rank).astype(jnp.int32)

def unit_rows(values):
    as_float = values.astype(jnp.float32)
    inverse = lax.rsqrt(lax.optimization_barrier(jnp.sum(as_float * as_float, axis=-1, keepdims=True)) + norm_eps)
    return (as_float * inverse, inverse)

def unit_back(normed, inverse, grad_normed):
    return inverse * (grad_normed - normed * lax.optimization_barrier(jnp.sum(normed * grad_normed, axis=-1, keepdims=True)))

def batch_pass(batch_args):
    query_block, passage_block, teacher_q_block, teacher_p_block, positive_block = batch_args
    query_unit, query_inv = unit_rows(query_block)
    passage_unit, passage_inv = unit_rows(passage_block)
    query_half = query_unit.astype(jnp.bfloat16)
    passage_half = passage_unit.astype(jnp.bfloat16)
    teacher_q_half = unit_rows(teacher_q_block)[0].astype(jnp.bfloat16)
    teacher_p_half = unit_rows(teacher_p_block)[0].astype(jnp.bfloat16)
    student = student_scale * jnp.dot(query_half, passage_half.T, preferred_element_type=jnp.float32)
    teacher = teacher_scale * jnp.dot(teacher_q_half, teacher_p_half.T, preferred_element_type=jnp.float32)
    student_exp = jnp.exp(student)
    teacher_exp = jnp.exp(teacher)
    student_total = lax.optimization_barrier(jnp.sum(student_exp, axis=1))
    teacher_total = lax.optimization_barrier(jnp.sum(teacher_exp, axis=1))
    cross_term = lax.optimization_barrier(jnp.sum(teacher_exp * (teacher - student), axis=1))
    is_positive = positive_block[:, None] == jnp.arange(PROWS, dtype=jnp.int32)[None, :]
    positive_score = lax.optimization_barrier(jnp.sum(jnp.where(is_positive, student, 0.0), axis=1))
    query_loss = 2.0 * jnp.log(student_total) - positive_score + cross_term / teacher_total - jnp.log(teacher_total)
    coeffs = (2.0 * student_exp / student_total[:, None] - teacher_exp / teacher_total[:, None] - is_positive.astype(jnp.float32)).astype(jnp.bfloat16)
    unit_q_grad = student_scale * jnp.dot(coeffs, passage_half, preferred_element_type=jnp.float32)
    unit_p_grad = student_scale * jnp.dot(coeffs.T, query_half, preferred_element_type=jnp.float32)
    return (query_loss, unit_back(query_unit, query_inv, unit_q_grad), unit_back(passage_unit, passage_inv, unit_p_grad))

def reference(tokens, expert_ids, gate_probs, w_gate, w_up, w_down, teacher_queries, teacher_passages, positives):
    gate_full = w_gate.astype(jnp.float32)
    up_full = w_up.astype(jnp.float32)
    down_full = w_down.astype(jnp.float32)
    group_tokens = TOK_DEV * N_EXPERT
    slot_total = EXPERTS * N_EXPERT * CAP

    def forward_group(group_args):
        tok_block, id_block, prob_block = group_args
        slot_index = slot_numbers(id_block)
        token_rep = jnp.repeat(tok_block, TOP, axis=0)
        rows_in = jnp.zeros((slot_total, D), jnp.bfloat16).at[slot_index].set(token_rep)
        expert_out = lax.map(expert_forward, (rows_in.reshape(EXPERTS, N_EXPERT * CAP, D), gate_full, up_full, down_full))
        token_out = expert_out.reshape(slot_total, D)[slot_index].astype(jnp.float32)
        prob_flat = prob_block.reshape(-1, 1).astype(jnp.float32)
        return lax.optimization_barrier(jnp.sum((prob_flat * token_out).reshape(group_tokens, TOP, D), axis=1)).astype(jnp.bfloat16)
    tok_groups = tokens.reshape(N_DP, group_tokens, D)
    id_groups = expert_ids.reshape(N_DP, group_tokens, TOP)
    prob_groups = gate_probs.reshape(N_DP, group_tokens, TOP)
    moe_out = lax.map(forward_group, (tok_groups, id_groups, prob_groups)).reshape(TOKENS, D)
    moe_blocks = moe_out.reshape(N_DP, N_EXPERT, TOK_DEV, D)
    query_tokens = moe_blocks[:, :, :Q_DEV * QLEN].reshape(N_DP, N_EXPERT, Q_DEV, QLEN, D)
    passage_tokens = moe_blocks[:, :, Q_DEV * QLEN:].reshape(N_DP, N_EXPERT, PASS_DEV, PLEN, D)
    pooled_q = lax.optimization_barrier(jnp.mean(query_tokens.astype(jnp.float32), axis=3))
    pooled_p = lax.optimization_barrier(jnp.mean(passage_tokens.astype(jnp.float32), axis=3))
    pooled_q = jnp.transpose(pooled_q, (1, 0, 2, 3)).reshape(BATCHES, QROWS, D)
    pooled_p = jnp.transpose(pooled_p, (1, 0, 2, 3)).reshape(BATCHES, PROWS, D)
    query_loss, query_grad, passage_grad = lax.map(batch_pass, (pooled_q, pooled_p, teacher_queries, teacher_passages, positives))
    q_grad_blocks = jnp.transpose(query_grad.reshape(BATCHES, N_DP, Q_DEV, D), (1, 0, 2, 3))
    p_grad_blocks = jnp.transpose(passage_grad.reshape(BATCHES, N_DP, PASS_DEV, D), (1, 0, 2, 3))

    def backward_group(group_args):
        tok_block, id_block, prob_block, q_grad_block, p_grad_block = group_args
        query_part = jnp.repeat(q_grad_block * (loss_scale / QLEN), QLEN, axis=1)
        passage_part = jnp.repeat(p_grad_block * (loss_scale / PLEN), PLEN, axis=1)
        out_grad = jnp.concatenate([query_part, passage_part], axis=1).reshape(group_tokens, D)
        slot_index = slot_numbers(id_block)
        token_rep = jnp.repeat(tok_block, TOP, axis=0)
        grad_rep = jnp.repeat(out_grad, TOP, axis=0)
        prob_flat = prob_block.reshape(-1, 1).astype(jnp.float32)
        routed_grad = (prob_flat * grad_rep).astype(jnp.bfloat16)
        rows_in = jnp.zeros((slot_total, D), jnp.bfloat16).at[slot_index].set(token_rep)
        grads_in = jnp.zeros((slot_total, D), jnp.bfloat16).at[slot_index].set(routed_grad)
        expert_out, row_grad = lax.map(expert_apply, (rows_in.reshape(EXPERTS, N_EXPERT * CAP, D), grads_in.reshape(EXPERTS, N_EXPERT * CAP, D), gate_full, up_full, down_full))
        token_out = expert_out.reshape(slot_total, D)[slot_index].astype(jnp.float32)
        token_row_grad = row_grad.reshape(slot_total, D)[slot_index].astype(jnp.float32)
        grad_block = lax.optimization_barrier(jnp.sum(token_row_grad.reshape(group_tokens, TOP, D), axis=1)).astype(jnp.bfloat16)
        gate_block = lax.optimization_barrier(jnp.sum(token_out * grad_rep, axis=1)).reshape(group_tokens, TOP)
        return (grad_block, gate_block)
    token_grad, gate_grad = lax.map(backward_group, (tok_groups, id_groups, prob_groups, q_grad_blocks, p_grad_blocks))
    token_grad = token_grad.reshape(TOKENS, D)
    gate_grad = gate_grad.reshape(TOKENS, TOP)
    return (moe_out, token_grad, gate_grad, query_loss)
```

```python
import functools

import jax
import jax.numpy as jnp
from jax import lax
from jax.experimental import pallas as pl
from jax.experimental.pallas import tpu as pltpu
from jax.sharding import PartitionSpec as P

QLEN = 32
PLEN = 48
student_scale = 50.0
teacher_scale = 80.0
loss_scale = 64.0
norm_eps = 1e-06
MESH = pl.DeviceIdType.MESH
F32 = jnp.float32
BF16 = jnp.bfloat16
LANES = 128


def mm(left, right):
    return jnp.dot(left, right, preferred_element_type=F32)


def mm_last(left, right):
    return lax.dot_general(left, right, (((1,), (1,)), ((), ())), preferred_element_type=F32)


def iota(shape, dim):
    return lax.broadcasted_iota(jnp.int32, shape, dim)


def unit_rows(values):
    inverse = lax.rsqrt(jnp.sum(values * values, axis=-1, keepdims=True) + norm_eps)
    return values * inverse, inverse


def kernel(
    dims,
    tok_ref, wg_hbm, wu_hbm, wd_hbm, ids_ref, probs_ref, tq_ref, tp_ref, pos_ref,
    moe_ref, tgrad_ref, ggrad_ref, loss_ref,
    xbuf, wg, wu, wd, c1, c2, hid, meta, wf, wt,
    cbuf, crecv, slab, tmine, smine, tgath, sgath, tmat, smat, unit_buf,
    ogmine, ogbuf, ogmat, hgpad, ggsend, ggrecv,
    s_a, r_a, s_b, r_b, s_c, r_c, keep0, keep2,
    send_sem, recv_sem, t_send, t_recv, s_send, s_recv, loc_sem,
):
    dp, ex, rows, width, ff, nq, npas, rp, tok_chunks, col_chunks = dims
    me = lax.axis_index("dp")
    my_e = lax.axis_index("expert")
    half = ex // 2
    sib = my_e + 1 - 2 * lax.rem(my_e, 2)
    cross = lax.rem(my_e + half, ex)
    xsib = lax.rem(sib + half, ex)
    peers = [None, sib, cross, xsib]
    chunk_rows = rows // tok_chunks
    dc = width // col_chunks
    counter = [0]
    started = []

    def remote(src, dst, target):
        at = counter[0]
        counter[0] += 1
        copy = pltpu.make_async_remote_copy(
            src_ref=src, dst_ref=dst, send_sem=send_sem.at[at], recv_sem=recv_sem.at[at],
            device_id=(me, target), device_id_type=MESH,
        )
        started.append(copy)
        return copy

    loads = [
        pltpu.make_async_copy(tok_ref, xbuf.at[pl.ds(0, rows)], loc_sem.at[0]),
        pltpu.make_async_copy(wg_hbm.at[0], wg, loc_sem.at[1]),
        pltpu.make_async_copy(wu_hbm.at[0], wu, loc_sem.at[2]),
        pltpu.make_async_copy(wd_hbm.at[0], wd, loc_sem.at[3]),
    ]
    for load in loads:
        load.start()

    barrier = pltpu.get_barrier_semaphore()
    for peer in peers[1:]:
        pl.semaphore_signal(barrier, inc=1, device_id=(me, peer), device_id_type=MESH)

    def greet(off, carry):
        pl.semaphore_signal(
            barrier, inc=1, device_id=(lax.rem(me + off, dp), my_e), device_id_type=MESH
        )
        return carry

    lax.fori_loop(1, dp, greet, 0)

    ids = ids_ref[...]
    probs = probs_ref[...].astype(F32)
    lane = iota((rows, LANES), 1)
    spread = jnp.zeros((rows, LANES), F32)
    for k in range(ids.shape[1]):
        spread += jnp.where(lane == ids[:, k : k + 1], probs[:, k : k + 1], 0.0)
    meta[0] = jnp.transpose(spread)[:8]

    slab[...] = jnp.zeros_like(slab)
    slab[0:nq, :] = unit_rows(tq_ref[0].astype(F32))[0]
    slab[nq : nq + npas, :] = unit_rows(tp_ref[0].astype(F32))[0]
    lane_row = iota((1, LANES), 1)
    pos_row = jnp.zeros((1, LANES), F32)
    for q in range(nq):
        value = pos_ref[0:1, q : q + 1]
        pos_row += jnp.where(lane_row == 2 * q, (value >> 6).astype(F32), 0.0)
        pos_row += jnp.where(lane_row == 2 * q + 1, (value & 63).astype(F32), 0.0)
    slab[nq + npas : nq + npas + 1, 0:LANES] = pos_row
    tmine[...] = slab[...].astype(BF16)

    pl.semaphore_wait(barrier, ex - 1 + dp - 1)

    token_copies = []
    for k in range(tok_chunks):
        at = pl.ds(k * chunk_rows, chunk_rows)
        to = pl.ds(2 * rows + k * chunk_rows, chunk_rows)
        token_copies.append(remote(tok_ref.at[at], xbuf.at[to], cross))
    sib_copy = remote(tok_ref, xbuf.at[pl.ds(rows, rows)], sib)
    meta_copies = [remote(meta.at[0], meta.at[s], peers[s]) for s in range(1, ex)]
    token_copies[0].start()
    sib_copy.start()
    for copy in meta_copies:
        copy.start()
    for copy in token_copies[1:]:
        copy.start()

    def spread_copy(off, src, gath, s_sem, r_sem, incoming):
        slot = lax.rem(me + dp - off, dp) if incoming else me
        return pltpu.make_async_remote_copy(
            src_ref=src, dst_ref=gath.at[slot], send_sem=s_sem.at[off], recv_sem=r_sem.at[off],
            device_id=(lax.rem(me + off, dp), my_e), device_id_type=MESH,
        )

    def spread_start(src, gath, s_sem, r_sem):
        def body(off, carry):
            spread_copy(off, src, gath, s_sem, r_sem, False).start()
            return carry

        lax.fori_loop(1, dp, body, 0)
        gath[me] = src[...]

    def spread_wait(src, gath, s_sem, r_sem):
        def body(off, carry):
            spread_copy(off, src, gath, s_sem, r_sem, True).wait_recv()
            return carry

        lax.fori_loop(1, dp, body, 0)

    def spread_done(src, gath, s_sem, r_sem):
        def body(off, carry):
            spread_copy(off, src, gath, s_sem, r_sem, False).wait_send()
            return carry

        lax.fori_loop(1, dp, body, 0)

    spread_start(tmine, tgath, t_send, t_recv)

    tile = 256 if ff % 256 == 0 else ff

    def forward(start, count):
        at = pl.ds(start, count)

        def body(i, carry):
            cols = pl.ds(pl.multiple_of(i * tile, tile), tile)
            values = xbuf[at, :]
            gate = mm(values, wg[:, cols])
            up = mm(values, wu[:, cols])
            sig = 1.0 / (1.0 + jnp.exp(-gate))
            act = gate * sig
            hid[at, cols] = (act * up).astype(BF16)
            c2[at, cols] = act
            c1[at, cols] = up * (sig * (1.0 + gate * (1.0 - sig)))
            return carry

        lax.fori_loop(0, ff // tile, body, 0)

    loads[0].wait()
    loads[1].wait()
    loads[2].wait()
    sib_copy.wait_recv()
    forward(0, 2 * rows)
    forward_copies = []
    for k in range(tok_chunks):
        token_copies[k].wait_recv()
        at = pl.ds(2 * rows + k * chunk_rows, chunk_rows)
        to = pl.ds(3 * rows + k * chunk_rows, chunk_rows)
        copy = remote(xbuf.at[at], xbuf.at[to], sib)
        copy.start()
        forward_copies.append(copy)

    for copy in meta_copies:
        copy.wait_recv()
    t_at = iota((rp, rows), 1)
    segment = jnp.where(t_at < nq * QLEN, t_at // QLEN, nq + (t_at - nq * QLEN) // PLEN)
    member = segment == iota((rp, rows), 0)
    wf[...] = jnp.zeros_like(wf)
    for s in range(ex):
        prow = jnp.sum(jnp.where(iota((8, rows), 0) == my_e, meta[s], 0.0), axis=0, keepdims=True)
        wf[s * rp : (s + 1) * rp, s * rows : (s + 1) * rows] = jnp.where(member, prow, 0.0)
    for s in range(ex):
        wt[s * rows : (s + 1) * rows, :] = jnp.transpose(wf[:, s * rows : (s + 1) * rows])
    loads[3].wait()

    for copy in forward_copies:
        copy.wait_recv()
    forward(2 * rows, 2 * rows)

    nseg = ex * rp
    pooled_hid = mm(wf[0:nseg, :].astype(BF16), hid[...])
    high = pooled_hid.astype(BF16)
    low = (pooled_hid - high.astype(F32)).astype(BF16)

    def pooled_cols(j, carry):
        cols = pl.ds(pl.multiple_of(j * dc, dc), dc)
        part = mm(high, wd[:, cols]) + mm(low, wd[:, cols])
        for s in range(ex):
            cbuf[s, :, cols] = part[s * rp : (s + 1) * rp, :]
        return carry

    lax.fori_loop(0, col_chunks, pooled_cols, 0)
    pooled_copies = [remote(cbuf.at[s], crecv.at[s], peers[s]) for s in range(1, ex)]
    for s in (2, 3, 1):
        pooled_copies[s - 1].start()

    pcol = jnp.sum(wt[...], axis=1, keepdims=True)

    def moe_cols(j, carry):
        cols = pl.ds(pl.multiple_of(j * dc, dc), dc)
        part = mm(hid[...], wd[:, cols]) * pcol
        keep0[0, j] = part[0:rows]
        s_c[0, j] = part[rows : 2 * rows].astype(BF16)
        keep2[j] = part[2 * rows : 3 * rows]
        s_a[0, j] = part[3 * rows :].astype(BF16)
        return carry

    lax.fori_loop(0, col_chunks, moe_cols, 0)
    moe_a = remote(s_a.at[0], r_a.at[0], sib)
    moe_c = remote(s_c.at[0], r_c.at[0], sib)
    moe_a.start()

    for copy in pooled_copies:
        copy.wait_recv()
    row_at = iota((rp, 1), 0)
    is_query = row_at < nq
    total = cbuf[0] + crecv[1] + crecv[2] + crecv[3]
    pooled = total * jnp.where(is_query, 1.0 / QLEN, 1.0 / PLEN)
    units, inverse = unit_rows(pooled)
    unit_buf[...] = units
    smine[...] = units.astype(BF16)
    spread_start(smine, sgath, s_send, s_recv)

    moe_c.start()
    moe_a.wait_recv()
    for j in range(col_chunks):
        s_b[0, j] = (keep2[j] + r_a[0, j].astype(F32)).astype(BF16)
    moe_b = [remote(s_b.at[0, j], r_b.at[0, j], cross) for j in range(col_chunks)]
    for copy in moe_b[: col_chunks // 2]:
        copy.start()

    spread_wait(tmine, tgath, t_send, t_recv)
    for i in range(dp):
        tmat[i * rp : (i + 1) * rp, :] = tgath[i].astype(F32)
    tall = tmat[...].astype(BF16)
    teacher = teacher_scale * mm_last(tall, tall)
    n = dp * rp
    row = iota((n, n), 0)
    col = iota((n, n), 1)
    col_in = col % rp
    is_row = (row % rp) < nq
    is_pass = jnp.logical_and(col_in >= nq, col_in < nq + npas)
    live = jnp.logical_and(is_row, is_pass)
    pad_row = jnp.where(col == (row // rp) * rp + nq + npas, 1.0, 0.0).astype(BF16)
    codes = mm(pad_row, tall[:, 0:LANES])
    code_lane = iota((n, LANES), 1)
    code_at = 2 * (iota((n, LANES), 0) % rp)
    positive = jnp.sum(
        jnp.where(code_lane == code_at, codes * 64.0, 0.0)
        + jnp.where(code_lane == code_at + 1, codes, 0.0),
        axis=1,
        keepdims=True,
    ).astype(jnp.int32)
    is_pos = jnp.logical_and(live, ((col // rp) * npas + col_in - nq) == positive)
    teacher = jnp.where(live, teacher, 0.0)
    teacher_exp = jnp.where(live, jnp.exp(teacher), 0.0)
    teacher_total = jnp.sum(teacher_exp, axis=1, keepdims=True)
    row_live = (iota((n, 1), 0) % rp) < nq
    teacher_total = jnp.where(row_live, teacher_total, 1.0)

    spread_wait(smine, sgath, s_send, s_recv)
    for i in range(dp):
        smat[i * rp : (i + 1) * rp, :] = sgath[i].astype(F32)
    sall = smat[...].astype(BF16)
    student = jnp.where(live, student_scale * mm_last(sall, sall), 0.0)
    student_exp = jnp.where(live, jnp.exp(student), 0.0)
    student_total = jnp.where(row_live, jnp.sum(student_exp, axis=1, keepdims=True), 1.0)
    crossed = jnp.sum(teacher_exp * (teacher - student), axis=1, keepdims=True)
    pos_score = jnp.sum(jnp.where(is_pos, student, 0.0), axis=1, keepdims=True)
    loss = (
        2.0 * jnp.log(student_total) - pos_score + crossed / teacher_total - jnp.log(teacher_total)
    )
    coeffs = (
        2.0 * student_exp / student_total
        - teacher_exp / teacher_total
        - jnp.where(is_pos, 1.0, 0.0)
    ).astype(BF16)
    pick = jnp.where(iota((8, n), 1) == me * rp + iota((8, n), 0), 1.0, 0.0)
    pick = jnp.where(iota((8, n), 0) < rp, pick, 0.0).astype(BF16)
    mine = mm(pick, coeffs) + mm_last(pick, coeffs)
    unit_grad = (student_scale * mm(mine.astype(BF16), sall))[0:rp]
    for q in range(nq):
        chosen = jnp.where(iota((n, 1), 0) == me * rp + q, loss, 0.0)
        loss_ref[0:1, q : q + 1] = jnp.sum(chosen, axis=0, keepdims=True)
    units = unit_buf[...]
    grad = inverse * (unit_grad - units * jnp.sum(units * unit_grad, axis=-1, keepdims=True))
    grad = grad * jnp.where(is_query, loss_scale / QLEN, loss_scale / PLEN)
    ogmine[...] = grad.astype(BF16)
    og_copies = [remote(ogmine, ogbuf.at[s], peers[s]) for s in range(1, ex)]
    for s in (2, 3, 1):
        og_copies[s - 1].start()
    for copy in moe_b[col_chunks // 2 :]:
        copy.start()

    hgpad[...] = jnp.zeros_like(hgpad)
    ogmat[0:rp, :] = grad
    for s in (1, 3, 2):
        og_copies[s - 1].wait_recv()
    for s in range(1, ex):
        ogmat[s * rp : (s + 1) * rp, :] = ogbuf[s].astype(F32)
    hg = mm_last(ogmat[...].astype(BF16), wd[...]).astype(BF16)
    hgpad[0:nseg, :] = hg
    gpart = c1
    upart = c2

    def back_rows(start, count):
        at = pl.ds(start, count)
        hidden_grad = mm(wt[at, :].astype(BF16), hgpad[...])
        gate_part = (hidden_grad * gpart[at, :]).astype(BF16)
        up_part = (hidden_grad * upart[at, :]).astype(BF16)
        return gate_part, up_part

    tg_a = [remote(s_a.at[1, j], r_a.at[1, j], sib) for j in range(col_chunks)]
    tg_b = [remote(s_b.at[1, j], r_b.at[1, j], cross) for j in range(col_chunks)]
    tg_c = [remote(s_c.at[1, j], r_c.at[1, j], sib) for j in range(col_chunks)]

    def combine(j):
        tg_a[j].wait_recv()
        s_b[1, j] = (keep2[j] + r_a[1, j].astype(F32)).astype(BF16)
        tg_b[j].start()

    gate_part, up_part = back_rows(2 * rows, 2 * rows)
    for j in range(col_chunks):
        at = pl.ds(j * dc, dc)
        part = mm_last(gate_part, wg[at, :]) + mm_last(up_part, wu[at, :])
        keep2[j] = part[0:rows]
        s_a[1, j] = part[rows:].astype(BF16)
        tg_a[j].start()
        if j:
            combine(j - 1)
    combine(col_chunks - 1)

    scores = mm_last(hg, hid[...])
    gg_copies = [remote(ggsend.at[s], ggrecv.at[s], peers[s]) for s in range(1, ex)]
    for s in range(ex):
        part = scores[s * rp : (s + 1) * rp, s * rows : (s + 1) * rows]
        line = jnp.sum(jnp.where(member, part, 0.0), axis=0, keepdims=True)
        ggsend[s] = jnp.where(iota((8, rows), 0) == my_e, line, 0.0)
    for copy in gg_copies:
        copy.start()

    gate_part, up_part = back_rows(0, 2 * rows)
    for j in range(col_chunks):
        at = pl.ds(j * dc, dc)
        part = mm_last(gate_part, wg[at, :]) + mm_last(up_part, wu[at, :])
        keep0[1, j] = part[0:rows]
        s_c[1, j] = part[rows:].astype(BF16)
        tg_c[j].start()

    moe_c.wait_recv()
    for j in range(col_chunks):
        moe_b[j].wait_recv()
        total = keep0[0, j] + r_c[0, j].astype(F32) + r_b[0, j].astype(F32)
        moe_ref[:, j * dc : (j + 1) * dc] = total.astype(BF16)
    for copy in gg_copies:
        copy.wait_recv()
    table = ggsend[0] + ggrecv[1] + ggrecv[2] + ggrecv[3]
    wf[0:8, 0:rows] = table
    table = jnp.transpose(wf[:, 0:rows])
    ids = ids_ref[...]
    for k in range(ids.shape[1]):
        chosen = jnp.where(lane == ids[:, k : k + 1], table, 0.0)
        ggrad_ref[:, k : k + 1] = jnp.sum(chosen, axis=1, keepdims=True)
    for j in range(col_chunks):
        tg_c[j].wait_recv()
        tg_b[j].wait_recv()
        total = keep0[1, j] + r_c[1, j].astype(F32) + r_b[1, j].astype(F32)
        tgrad_ref[:, j * dc : (j + 1) * dc] = total.astype(BF16)

    for copy in started:
        copy.wait_send()
    spread_done(tmine, tgath, t_send, t_recv)
    spread_done(smine, sgath, s_send, s_recv)


def shards(
    dp, ex,
    tokens, expert_ids, gate_probs, w_gate, w_up, w_down, teacher_queries, teacher_passages, positives,
):
    rows, width = tokens.shape
    ff = w_gate.shape[2]
    nq = teacher_queries.shape[1]
    npas = teacher_passages.shape[1]
    rp = -(-(nq + npas + 1) // 4) * 4
    tok_chunks, col_chunks = 4, 4
    dc = width // col_chunks
    dims = (dp, ex, rows, width, ff, nq, npas, rp, tok_chunks, col_chunks)
    copies = 2 * tok_chunks + 1 + 4 * (ex - 1) + 2 + col_chunks + 3 * col_chunks
    vmem = pl.BlockSpec(memory_space=pltpu.VMEM)
    hbm = pl.BlockSpec(memory_space=pl.ANY)
    dma = pltpu.SemaphoreType.DMA
    moved = pltpu.VMEM((2, col_chunks, rows, dc), BF16)
    moe, tgrad, ggrad, loss = pl.pallas_call(
        functools.partial(kernel, dims),
        out_shape=(
            jax.ShapeDtypeStruct((rows, width), BF16),
            jax.ShapeDtypeStruct((rows, width), BF16),
            jax.ShapeDtypeStruct(expert_ids.shape, F32),
            jax.ShapeDtypeStruct((1, nq), F32),
        ),
        in_specs=[hbm] * 4 + [vmem] * 5,
        out_specs=(vmem,) * 4,
        scratch_shapes=[
            pltpu.VMEM((ex * rows, width), BF16),
            pltpu.VMEM((width, ff), BF16),
            pltpu.VMEM((width, ff), BF16),
            pltpu.VMEM((ff, width), BF16),
            pltpu.VMEM((ex * rows, ff), F32),
            pltpu.VMEM((ex * rows, ff), F32),
            pltpu.VMEM((ex * rows, ff), BF16),
            pltpu.VMEM((ex, 8, rows), F32),
            pltpu.VMEM((LANES, ex * rows), F32),
            pltpu.VMEM((ex * rows, LANES), F32),
            pltpu.VMEM((ex, rp, width), F32),
            pltpu.VMEM((ex, rp, width), F32),
            pltpu.VMEM((rp, width), F32),
            pltpu.VMEM((rp, width), BF16),
            pltpu.VMEM((rp, width), BF16),
            pltpu.VMEM((dp, rp, width), BF16),
            pltpu.VMEM((dp, rp, width), BF16),
            pltpu.VMEM((dp * rp, width), F32),
            pltpu.VMEM((dp * rp, width), F32),
            pltpu.VMEM((rp, width), F32),
            pltpu.VMEM((rp, width), BF16),
            pltpu.VMEM((ex, rp, width), BF16),
            pltpu.VMEM((ex * rp, width), F32),
            pltpu.VMEM((LANES, ff), BF16),
            pltpu.VMEM((ex, 8, rows), F32),
            pltpu.VMEM((ex, 8, rows), F32),
            moved, moved, moved, moved, moved, moved,
            pltpu.VMEM((2, col_chunks, rows, dc), F32),
            pltpu.VMEM((col_chunks, rows, dc), F32),
            dma((copies,)), dma((copies,)),
            dma((dp,)), dma((dp,)), dma((dp,)), dma((dp,)),
            dma((4,)),
        ],
        compiler_params=pltpu.CompilerParams(
            collective_id=0, has_side_effects=True, vmem_limit_bytes=60 * 1024 * 1024
        ),
    )(
        tokens, w_gate, w_up, w_down, expert_ids, gate_probs,
        teacher_queries, teacher_passages, positives,
    )
    return moe, tgrad, ggrad, loss


def solution(mesh):
    in_specs = (
        P(("dp", "expert"), None),
        P(("dp", "expert"), None),
        P(("dp", "expert"), None),
        P("expert", None, None),
        P("expert", None, None),
        P("expert", None, None),
        P("expert", "dp", None),
        P("expert", "dp", None),
        P("expert", "dp"),
    )
    out_specs = (
        P(("dp", "expert"), None),
        P(("dp", "expert"), None),
        P(("dp", "expert"), None),
        P("expert", "dp"),
    )
    body = functools.partial(shards, mesh.shape["dp"], mesh.shape["expert"])
    return jax.shard_map(body, mesh=mesh, in_specs=in_specs, out_specs=out_specs, check_vma=False)
```

```python
import functools

import jax
import jax.numpy as jnp
from jax import lax
from jax.experimental import pallas as pl
from jax.experimental.pallas import tpu as pltpu
from jax.sharding import PartitionSpec as P

QLEN = 32
PLEN = 48
student_scale = 50.0
teacher_scale = 80.0
loss_scale = 64.0
norm_eps = 1e-06
MESH = pl.DeviceIdType.MESH
F32 = jnp.float32
BF16 = jnp.bfloat16
LANES = 128


def mm(left, right):
    return jnp.dot(left, right, preferred_element_type=F32)


def mm_last(left, right):
    return lax.dot_general(left, right, (((1,), (1,)), ((), ())), preferred_element_type=F32)


def iota(shape, dim):
    return lax.broadcasted_iota(jnp.int32, shape, dim)


def unit_rows(values):
    inverse = lax.rsqrt(jnp.sum(values * values, axis=-1, keepdims=True) + norm_eps)
    return values * inverse, inverse


def kernel(
    dims,
    tok_ref, wg_hbm, wu_hbm, wd_hbm, ids_ref, probs_ref, tq_ref, tp_ref, pos_ref,
    moe_ref, tgrad_ref, ggrad_ref, loss_ref,
    xbuf, wg, wu, wd, c1, c2, hid, meta, wf, wt,
    cbuf, crecv, slab, tmine, smine, tgath, sgath, tmat, smat, unit_buf,
    ogmine, ogbuf, ogmat, hgpad, ggsend, ggrecv,
    s_a, r_a, s_b, r_b, s_c, r_c, keep0, keep2,
    out_v, send_sem, recv_sem, t_send, t_recv, s_send, s_recv, loc_sem, out_sem,
):
    dp, ex, rows, width, ff, nq, npas, rp, tok_chunks, col_chunks = dims
    me = lax.axis_index("dp")
    my_e = lax.axis_index("expert")
    half = ex // 2
    sib = my_e + 1 - 2 * lax.rem(my_e, 2)
    cross = lax.rem(my_e + half, ex)
    xsib = lax.rem(sib + half, ex)
    peers = [None, sib, cross, xsib]
    chunk_rows = rows // tok_chunks
    part_rows = rows // 2
    places = [
        [(0, rows, 0)],
        [(rows, rows, 0)],
        [(2 * rows, part_rows, 0), (3 * rows, part_rows, part_rows)],
        [(2 * rows + part_rows, part_rows, 0), (3 * rows + part_rows, part_rows, part_rows)],
    ]

    def far(slot, k):
        token = k * chunk_rows
        return 2 * rows + (token // part_rows) * rows + (slot - 2) * part_rows + token % part_rows

    dc = width // col_chunks
    counter = [0]
    started = []

    def remote(src, dst, target):
        at = counter[0]
        counter[0] += 1
        copy = pltpu.make_async_remote_copy(
            src_ref=src, dst_ref=dst, send_sem=send_sem.at[at], recv_sem=recv_sem.at[at],
            device_id=(me, target), device_id_type=MESH,
        )
        started.append(copy)
        return copy

    loads = [
        pltpu.make_async_copy(tok_ref, xbuf.at[pl.ds(0, rows)], loc_sem.at[0]),
        pltpu.make_async_copy(wg_hbm.at[0], wg, loc_sem.at[1]),
        pltpu.make_async_copy(wu_hbm.at[0], wu, loc_sem.at[2]),
        pltpu.make_async_copy(wd_hbm.at[0], wd, loc_sem.at[3]),
    ]
    for load in loads:
        load.start()

    barrier = pltpu.get_barrier_semaphore()
    for peer in peers[1:]:
        pl.semaphore_signal(barrier, inc=1, device_id=(me, peer), device_id_type=MESH)

    def greet(off, carry):
        pl.semaphore_signal(
            barrier, inc=1, device_id=(lax.rem(me + off, dp), my_e), device_id_type=MESH
        )
        return carry

    lax.fori_loop(1, dp, greet, 0)

    ids = ids_ref[...]
    probs = probs_ref[...].astype(F32)
    lane = iota((8, rows), 0)
    spread = jnp.zeros((8, rows), F32)
    for k in range(ids.shape[0]):
        spread += jnp.where(lane == ids[k : k + 1, :], probs[k : k + 1, :], 0.0)
    meta[0] = spread

    slab[...] = jnp.zeros_like(slab)
    slab[0:nq, :] = unit_rows(tq_ref[0].astype(F32))[0]
    slab[nq : nq + npas, :] = unit_rows(tp_ref[0].astype(F32))[0]
    lane_row = iota((1, LANES), 1)
    pos_row = jnp.zeros((1, LANES), F32)
    for q in range(nq):
        value = pos_ref[0:1, q : q + 1]
        pos_row += jnp.where(lane_row == 2 * q, (value >> 6).astype(F32), 0.0)
        pos_row += jnp.where(lane_row == 2 * q + 1, (value & 63).astype(F32), 0.0)
    slab[nq + npas : nq + npas + 1, 0:LANES] = pos_row
    tmine[...] = slab[...].astype(BF16)

    pl.semaphore_wait(barrier, ex - 1 + dp - 1)

    token_copies = []
    for k in range(tok_chunks):
        at = pl.ds(k * chunk_rows, chunk_rows)
        to = pl.ds(far(2, k), chunk_rows)
        token_copies.append(remote(tok_ref.at[at], xbuf.at[to], cross))
    sib_copy = remote(tok_ref, xbuf.at[pl.ds(rows, rows)], sib)
    meta_copies = [remote(meta.at[0], meta.at[s], peers[s]) for s in range(1, ex)]
    token_copies[0].start()
    sib_copy.start()
    for copy in meta_copies:
        copy.start()
    for copy in token_copies[1:]:
        copy.start()

    def spread_copy(off, src, gath, s_sem, r_sem, incoming):
        slot = lax.rem(me + dp - off, dp) if incoming else me
        return pltpu.make_async_remote_copy(
            src_ref=src, dst_ref=gath.at[slot], send_sem=s_sem.at[off], recv_sem=r_sem.at[off],
            device_id=(lax.rem(me + off, dp), my_e), device_id_type=MESH,
        )

    def spread_start(src, gath, s_sem, r_sem):
        def body(off, carry):
            spread_copy(off, src, gath, s_sem, r_sem, False).start()
            return carry

        lax.fori_loop(1, dp, body, 0)
        gath[me] = src[...]

    def spread_wait(src, gath, s_sem, r_sem):
        def body(off, carry):
            spread_copy(off, src, gath, s_sem, r_sem, True).wait_recv()
            return carry

        lax.fori_loop(1, dp, body, 0)

    def spread_done(src, gath, s_sem, r_sem):
        def body(off, carry):
            spread_copy(off, src, gath, s_sem, r_sem, False).wait_send()
            return carry

        lax.fori_loop(1, dp, body, 0)

    spread_start(tmine, tgath, t_send, t_recv)

    tile = 256 if ff % 256 == 0 else ff

    def forward(start, count):
        at = pl.ds(start, count)

        def body(i, carry):
            cols = pl.ds(pl.multiple_of(i * tile, tile), tile)
            values = xbuf[at, :]
            gate = mm(values, wg[:, cols])
            up = mm(values, wu[:, cols])
            sig = 1.0 / (1.0 + jnp.exp(-gate))
            act = gate * sig
            hid[at, cols] = (act * up).astype(BF16)
            c2[at, cols] = act
            c1[at, cols] = up * (sig * (1.0 + gate * (1.0 - sig)))
            return carry

        lax.fori_loop(0, ff // tile, body, 0)

    loads[0].wait()
    loads[1].wait()
    loads[2].wait()
    sib_copy.wait_recv()
    forward(0, 2 * rows)
    forward_copies = []
    for k in range(tok_chunks):
        token_copies[k].wait_recv()
        copy = remote(
            xbuf.at[pl.ds(far(2, k), chunk_rows)], xbuf.at[pl.ds(far(3, k), chunk_rows)], sib
        )
        copy.start()
        forward_copies.append(copy)
        if k == tok_chunks // 2 - 1:
            for copy in forward_copies:
                copy.wait_recv()
            forward(2 * rows, rows)

    for copy in meta_copies:
        copy.wait_recv()
    t_at = iota((rp, rows), 1)
    segment = jnp.where(t_at < nq * QLEN, t_at // QLEN, nq + (t_at - nq * QLEN) // PLEN)
    member = segment == iota((rp, rows), 0)
    wf[...] = jnp.zeros_like(wf)
    for s in range(ex):
        prow = jnp.sum(jnp.where(iota((8, rows), 0) == my_e, meta[s], 0.0), axis=0, keepdims=True)
        weights = jnp.where(member, prow, 0.0)
        for start, count, token in places[s]:
            wf[s * rp : (s + 1) * rp, start : start + count] = weights[:, token : token + count]
    for s in range(ex):
        wt[s * rows : (s + 1) * rows, :] = jnp.transpose(wf[:, s * rows : (s + 1) * rows])
    loads[3].wait()

    for copy in forward_copies[tok_chunks // 2 :]:
        copy.wait_recv()
    forward(3 * rows, rows)

    nseg = ex * rp
    pooled_hid = mm(wf[0:nseg, :].astype(BF16), hid[...])
    high = pooled_hid.astype(BF16)
    low = (pooled_hid - high.astype(F32)).astype(BF16)
    both = jnp.concatenate([high, low], axis=0)

    def pooled_cols(j, carry):
        cols = pl.ds(pl.multiple_of(j * dc, dc), dc)
        part = mm(both, wd[:, cols])
        part = part[0:nseg] + part[nseg:]
        for s in range(ex):
            cbuf[s, :, cols] = part[s * rp : (s + 1) * rp, :].astype(BF16)
        return carry

    lax.fori_loop(0, col_chunks, pooled_cols, 0)
    pooled_copies = [remote(cbuf.at[s], crecv.at[s], peers[s]) for s in range(1, ex)]
    for s in (2, 3, 1):
        pooled_copies[s - 1].start()

    pcol = jnp.sum(wt[...], axis=1, keepdims=True)

    moe_a = [remote(s_a.at[0, j], r_a.at[0, j], sib) for j in range(col_chunks)]
    moe_b = [remote(s_b.at[0, j], r_b.at[0, j], cross) for j in range(col_chunks)]
    moe_c = remote(s_c.at[0], r_c.at[0], sib)

    def moe_part(j):
        part = mm(hid[...], wd[:, j * dc : (j + 1) * dc]) * pcol
        keep0[0, j] = part[0:rows]
        s_c[0, j] = part[rows : 2 * rows].astype(BF16)
        for start, count, token in places[2]:
            keep2[j, token : token + count] = part[start : start + count]
        for start, count, token in places[3]:
            s_a[0, j, token : token + count] = part[start : start + count].astype(BF16)
        moe_a[j].start()

    def moe_combine(j):
        moe_a[j].wait_recv()
        s_b[0, j] = (keep2[j] + r_a[0, j].astype(F32)).astype(BF16)

    early = col_chunks // 2
    for j in range(early + 1):
        moe_part(j)
        if j:
            moe_combine(j - 1)
            moe_b[j - 1].start()

    for copy in pooled_copies:
        copy.wait_recv()
    row_at = iota((rp, 1), 0)
    is_query = row_at < nq
    total = cbuf[0].astype(F32)
    for s in range(1, ex):
        total += crecv[s].astype(F32)
    pooled = total * jnp.where(is_query, 1.0 / QLEN, 1.0 / PLEN)
    units, inverse = unit_rows(pooled)
    unit_buf[...] = units
    smine[...] = units.astype(BF16)
    spread_start(smine, sgath, s_send, s_recv)

    for j in range(early + 1, col_chunks):
        moe_part(j)
    moe_c.start()
    for j in range(early, col_chunks):
        moe_combine(j)

    spread_wait(tmine, tgath, t_send, t_recv)
    for i in range(dp):
        tmat[i * rp : (i + 1) * rp, :] = tgath[i].astype(F32)
    tall = tmat[...].astype(BF16)
    teacher = teacher_scale * mm_last(tall, tall)
    n = dp * rp
    row = iota((n, n), 0)
    col = iota((n, n), 1)
    col_in = col % rp
    is_row = (row % rp) < nq
    is_pass = jnp.logical_and(col_in >= nq, col_in < nq + npas)
    live = jnp.logical_and(is_row, is_pass)
    pad_row = jnp.where(col == (row // rp) * rp + nq + npas, 1.0, 0.0).astype(BF16)
    codes = mm(pad_row, tall[:, 0:LANES])
    code_lane = iota((n, LANES), 1)
    code_at = 2 * (iota((n, LANES), 0) % rp)
    positive = jnp.sum(
        jnp.where(code_lane == code_at, codes * 64.0, 0.0)
        + jnp.where(code_lane == code_at + 1, codes, 0.0),
        axis=1,
        keepdims=True,
    ).astype(jnp.int32)
    is_pos = jnp.logical_and(live, ((col // rp) * npas + col_in - nq) == positive)
    teacher = jnp.where(live, teacher, 0.0)
    teacher_exp = jnp.where(live, jnp.exp(teacher), 0.0)
    teacher_total = jnp.sum(teacher_exp, axis=1, keepdims=True)
    row_live = (iota((n, 1), 0) % rp) < nq
    teacher_total = jnp.where(row_live, teacher_total, 1.0)

    spread_wait(smine, sgath, s_send, s_recv)
    for i in range(dp):
        smat[i * rp : (i + 1) * rp, :] = sgath[i].astype(F32)
    sall = smat[...].astype(BF16)
    student = jnp.where(live, student_scale * mm_last(sall, sall), 0.0)
    student_exp = jnp.where(live, jnp.exp(student), 0.0)
    student_total = jnp.where(row_live, jnp.sum(student_exp, axis=1, keepdims=True), 1.0)
    crossed = jnp.sum(teacher_exp * (teacher - student), axis=1, keepdims=True)
    pos_score = jnp.sum(jnp.where(is_pos, student, 0.0), axis=1, keepdims=True)
    loss = (
        2.0 * jnp.log(student_total) - pos_score + crossed / teacher_total - jnp.log(teacher_total)
    )
    coeffs = (
        2.0 * student_exp / student_total
        - teacher_exp / teacher_total
        - jnp.where(is_pos, 1.0, 0.0)
    ).astype(BF16)
    pick = jnp.where(iota((8, n), 1) == me * rp + iota((8, n), 0), 1.0, 0.0)
    pick = jnp.where(iota((8, n), 0) < rp, pick, 0.0).astype(BF16)
    mine = mm(pick, coeffs) + mm_last(pick, coeffs)
    unit_grad = (student_scale * mm(mine.astype(BF16), sall))[0:rp]
    for q in range(nq):
        chosen = jnp.where(iota((n, 1), 0) == me * rp + q, loss, 0.0)
        loss_ref[0:1, q : q + 1] = jnp.sum(chosen, axis=0, keepdims=True)
    units = unit_buf[...]
    grad = inverse * (unit_grad - units * jnp.sum(units * unit_grad, axis=-1, keepdims=True))
    grad = grad * jnp.where(is_query, loss_scale / QLEN, loss_scale / PLEN)
    ogmine[...] = grad.astype(BF16)
    og_copies = [remote(ogmine, ogbuf.at[s], peers[s]) for s in range(1, ex)]
    for s in (2, 3, 1):
        og_copies[s - 1].start()
    for copy in moe_b[early:]:
        copy.start()

    hgpad[...] = jnp.zeros_like(hgpad)
    ogmat[0:rp, :] = grad
    for s in (1, 3, 2):
        og_copies[s - 1].wait_recv()
    for s in range(1, ex):
        ogmat[s * rp : (s + 1) * rp, :] = ogbuf[s].astype(F32)
    hg = mm_last(ogmat[...].astype(BF16), wd[...]).astype(BF16)
    hgpad[0:nseg, :] = hg
    gpart = c1
    upart = c2

    def back_rows(start, count):
        at = pl.ds(start, count)
        hidden_grad = mm(wt[at, :].astype(BF16), hgpad[...])
        gate_part = (hidden_grad * gpart[at, :]).astype(BF16)
        up_part = (hidden_grad * upart[at, :]).astype(BF16)
        return gate_part, up_part

    tg_a = [remote(s_a.at[1, j], r_a.at[1, j], sib) for j in range(col_chunks)]
    tg_b = [remote(s_b.at[1, j], r_b.at[1, j], cross) for j in range(col_chunks)]
    tg_c = [remote(s_c.at[1, j], r_c.at[1, j], sib) for j in range(col_chunks)]

    def combine(j):
        tg_a[j].wait_recv()
        s_b[1, j] = (keep2[j] + r_a[1, j].astype(F32)).astype(BF16)
        tg_b[j].start()

    gate_part, up_part = back_rows(2 * rows, 2 * rows)
    for j in range(col_chunks):
        at = pl.ds(j * dc, dc)
        part = mm_last(gate_part, wg[at, :]) + mm_last(up_part, wu[at, :])
        for start, count, token in places[2]:
            keep2[j, token : token + count] = part[start - 2 * rows : start - 2 * rows + count]
        for start, count, token in places[3]:
            shifted = part[start - 2 * rows : start - 2 * rows + count]
            s_a[1, j, token : token + count] = shifted.astype(BF16)
        tg_a[j].start()
        if j:
            combine(j - 1)
    combine(col_chunks - 1)

    scores = mm_last(hg, hid[...])
    gg_copies = [remote(ggsend.at[s], ggrecv.at[s], peers[s]) for s in range(1, ex)]
    for s in range(ex):
        part = jnp.concatenate(
            [scores[s * rp : (s + 1) * rp, start : start + count] for start, count, _ in places[s]],
            axis=1,
        )
        line = jnp.sum(jnp.where(member, part, 0.0), axis=0, keepdims=True)
        ggsend[s] = jnp.where(iota((8, rows), 0) == my_e, line, 0.0)
    for copy in gg_copies:
        copy.start()

    gate_part, up_part = back_rows(0, 2 * rows)
    for j in range(col_chunks):
        at = pl.ds(j * dc, dc)
        part = mm_last(gate_part, wg[at, :]) + mm_last(up_part, wu[at, :])
        keep0[1, j] = part[0:rows]
        s_c[1, j] = part[rows:].astype(BF16)
        tg_c[j].start()

    writes = []

    def write(which, j, target):
        cols = pl.ds(j * dc, dc)
        copy = pltpu.make_async_copy(
            out_v.at[which, :, cols], target.at[:, cols], out_sem.at[which, j]
        )
        copy.start()
        writes.append(copy)

    moe_c.wait_recv()
    for j in range(col_chunks):
        moe_b[j].wait_recv()
        total = keep0[0, j] + r_c[0, j].astype(F32) + r_b[0, j].astype(F32)
        out_v[0, :, j * dc : (j + 1) * dc] = total.astype(BF16)
        write(0, j, moe_ref)
    for copy in gg_copies:
        copy.wait_recv()
    table = ggsend[0] + ggrecv[1] + ggrecv[2] + ggrecv[3]
    ids = ids_ref[...]
    for k in range(ids.shape[0]):
        chosen = jnp.where(lane == ids[k : k + 1, :], table, 0.0)
        ggrad_ref[k : k + 1, :] = jnp.sum(chosen, axis=0, keepdims=True)
    for j in range(col_chunks):
        tg_c[j].wait_recv()
        tg_b[j].wait_recv()
        total = keep0[1, j] + r_c[1, j].astype(F32) + r_b[1, j].astype(F32)
        out_v[1, :, j * dc : (j + 1) * dc] = total.astype(BF16)
        write(1, j, tgrad_ref)

    for copy in started:
        copy.wait_send()
    for copy in writes:
        copy.wait()
    spread_done(tmine, tgath, t_send, t_recv)
    spread_done(smine, sgath, s_send, s_recv)


def hand_on(moe_in, tgrad_in, ggrad_in, loss_in, moe, tgrad, ggrad, loss, sem):
    copies = [
        pltpu.make_async_copy(moe_in, moe, sem.at[0]),
        pltpu.make_async_copy(tgrad_in, tgrad, sem.at[1]),
    ]
    for copy in copies:
        copy.start()
    ggrad[...] = ggrad_in[...]
    loss[...] = loss_in[...]
    for copy in copies:
        copy.wait()


def shards(
    dp, ex,
    tokens, expert_ids, gate_probs, w_gate, w_up, w_down, teacher_queries, teacher_passages, positives,
):
    rows, width = tokens.shape
    ff = w_gate.shape[2]
    nq = teacher_queries.shape[1]
    npas = teacher_passages.shape[1]
    rp = -(-(nq + npas + 1) // 4) * 4
    tok_chunks, col_chunks = 4, 4
    dc = width // col_chunks
    dims = (dp, ex, rows, width, ff, nq, npas, rp, tok_chunks, col_chunks)
    copies = 2 * tok_chunks + 1 + 4 * (ex - 1) + 1 + 2 * col_chunks + 3 * col_chunks
    vmem = pl.BlockSpec(memory_space=pltpu.VMEM)
    hbm = pl.BlockSpec(memory_space=pl.ANY)
    dma = pltpu.SemaphoreType.DMA
    moved = pltpu.VMEM((2, col_chunks, rows, dc), BF16)
    moe, tgrad, ggrad, loss = pl.pallas_call(
        functools.partial(kernel, dims),
        out_shape=(
            jax.ShapeDtypeStruct((rows, width), BF16),
            jax.ShapeDtypeStruct((rows, width), BF16),
            jax.ShapeDtypeStruct(expert_ids.shape[::-1], F32),
            jax.ShapeDtypeStruct((1, nq), F32),
        ),
        in_specs=[hbm] * 4 + [vmem] * 5,
        out_specs=(hbm, hbm, vmem, vmem),
        scratch_shapes=[
            pltpu.VMEM((ex * rows, width), BF16),
            pltpu.VMEM((width, ff), BF16),
            pltpu.VMEM((width, ff), BF16),
            pltpu.VMEM((ff, width), BF16),
            pltpu.VMEM((ex * rows, ff), F32),
            pltpu.VMEM((ex * rows, ff), F32),
            pltpu.VMEM((ex * rows, ff), BF16),
            pltpu.VMEM((ex, 8, rows), F32),
            pltpu.VMEM((LANES, ex * rows), F32),
            pltpu.VMEM((ex * rows, LANES), F32),
            pltpu.VMEM((ex, rp, width), BF16),
            pltpu.VMEM((ex, rp, width), BF16),
            pltpu.VMEM((rp, width), F32),
            pltpu.VMEM((rp, width), BF16),
            pltpu.VMEM((rp, width), BF16),
            pltpu.VMEM((dp, rp, width), BF16),
            pltpu.VMEM((dp, rp, width), BF16),
            pltpu.VMEM((dp * rp, width), F32),
            pltpu.VMEM((dp * rp, width), F32),
            pltpu.VMEM((rp, width), F32),
            pltpu.VMEM((rp, width), BF16),
            pltpu.VMEM((ex, rp, width), BF16),
            pltpu.VMEM((ex * rp, width), F32),
            pltpu.VMEM((LANES, ff), BF16),
            pltpu.VMEM((ex, 8, rows), F32),
            pltpu.VMEM((ex, 8, rows), F32),
            moved, moved, moved, moved, moved, moved,
            pltpu.VMEM((2, col_chunks, rows, dc), F32),
            pltpu.VMEM((col_chunks, rows, dc), F32),
            pltpu.VMEM((2, rows, width), BF16),
            dma((copies,)), dma((copies,)),
            dma((dp,)), dma((dp,)), dma((dp,)), dma((dp,)),
            dma((4,)), dma((2, col_chunks)),
        ],
        compiler_params=pltpu.CompilerParams(
            collective_id=0, has_side_effects=True, vmem_limit_bytes=60 * 1024 * 1024
        ),
    )(
        tokens, w_gate, w_up, w_down, expert_ids.T, gate_probs.T,
        teacher_queries, teacher_passages, positives,
    )
    moe, tgrad, ggrad, loss = pl.pallas_call(
        hand_on,
        out_shape=tuple(jax.ShapeDtypeStruct(a.shape, a.dtype) for a in (moe, tgrad, ggrad, loss)),
        in_specs=[hbm, hbm, vmem, vmem],
        out_specs=(hbm, hbm, vmem, vmem),
        scratch_shapes=[dma((2,))],
        compiler_params=pltpu.CompilerParams(vmem_limit_bytes=60 * 1024 * 1024),
    )(moe, tgrad, ggrad, loss)
    return moe, tgrad, ggrad.T, loss


def solution(mesh):
    in_specs = (
        P(("dp", "expert"), None),
        P(("dp", "expert"), None),
        P(("dp", "expert"), None),
        P("expert", None, None),
        P("expert", None, None),
        P("expert", None, None),
        P("expert", "dp", None),
        P("expert", "dp", None),
        P("expert", "dp"),
    )
    out_specs = (
        P(("dp", "expert"), None),
        P(("dp", "expert"), None),
        P(("dp", "expert"), None),
        P("expert", "dp"),
    )
    body = functools.partial(shards, mesh.shape["dp"], mesh.shape["expert"])
    return jax.shard_map(body, mesh=mesh, in_specs=in_specs, out_specs=out_specs, check_vma=False)
```

```python
import functools

import jax
import jax.numpy as jnp
from jax import lax
from jax.experimental import pallas as pl
from jax.experimental.pallas import tpu as pltpu
from jax.sharding import PartitionSpec as P

QLEN = 32
PLEN = 48
student_scale = 50.0
teacher_scale = 80.0
loss_scale = 64.0
norm_eps = 1e-06
MESH = pl.DeviceIdType.MESH
F32 = jnp.float32
BF16 = jnp.bfloat16
LANES = 128


def mm(left, right):
    return jnp.dot(left, right, preferred_element_type=F32)


def mm_last(left, right):
    return lax.dot_general(left, right, (((1,), (1,)), ((), ())), preferred_element_type=F32)


def iota(shape, dim):
    return lax.broadcasted_iota(jnp.int32, shape, dim)


def unit_rows(values):
    inverse = lax.rsqrt(jnp.sum(values * values, axis=-1, keepdims=True) + norm_eps)
    return values * inverse, inverse


def kernel(
    dims,
    tok_ref, wg_hbm, wu_hbm, wd_hbm, ids_ref, probs_ref, tq_ref, tp_ref, pos_ref,
    moe_ref, tgrad_ref, ggrad_ref, loss_ref,
    xbuf, wg, wu, wd, c1, c2, hid, meta, wf, wt,
    cbuf, crecv, slab, tmine, smine, tgath, sgath, tmat, smat, unit_buf,
    ogmine, ogbuf, ogmat, hgpad, ggsend, ggrecv,
    s_a, r_a, s_b, r_b, s_c, r_c, keep0, keep2,
    out_v, send_sem, recv_sem, t_send, t_recv, s_send, s_recv, loc_sem, out_sem,
):
    dp, ex, rows, width, ff, nq, npas, rp, tok_chunks, col_chunks = dims
    me = lax.axis_index("dp")
    my_e = lax.axis_index("expert")
    half = ex // 2
    sib = my_e + 1 - 2 * lax.rem(my_e, 2)
    cross = lax.rem(my_e + half, ex)
    xsib = lax.rem(sib + half, ex)
    peers = [None, sib, cross, xsib]
    chunk_rows = rows // tok_chunks
    part_rows = rows // 2
    places = [
        [(0, rows, 0)],
        [(rows, rows, 0)],
        [(2 * rows, part_rows, 0), (3 * rows, part_rows, part_rows)],
        [(2 * rows + part_rows, part_rows, 0), (3 * rows + part_rows, part_rows, part_rows)],
    ]

    def far(slot, k):
        token = k * chunk_rows
        return 2 * rows + (token // part_rows) * rows + (slot - 2) * part_rows + token % part_rows

    dc = width // col_chunks
    counter = [0]
    started = []

    def remote(src, dst, target):
        at = counter[0]
        counter[0] += 1
        copy = pltpu.make_async_remote_copy(
            src_ref=src, dst_ref=dst, send_sem=send_sem.at[at], recv_sem=recv_sem.at[at],
            device_id=(me, target), device_id_type=MESH,
        )
        started.append(copy)
        return copy

    loads = [
        pltpu.make_async_copy(tok_ref, xbuf.at[pl.ds(0, rows)], loc_sem.at[0]),
        pltpu.make_async_copy(wg_hbm.at[0], wg, loc_sem.at[1]),
        pltpu.make_async_copy(wu_hbm.at[0], wu, loc_sem.at[2]),
        pltpu.make_async_copy(wd_hbm.at[0], wd, loc_sem.at[3]),
    ]
    for load in loads:
        load.start()

    barrier = pltpu.get_barrier_semaphore()
    for peer in peers[1:]:
        pl.semaphore_signal(barrier, inc=1, device_id=(me, peer), device_id_type=MESH)

    def greet(off, carry):
        pl.semaphore_signal(
            barrier, inc=1, device_id=(lax.rem(me + off, dp), my_e), device_id_type=MESH
        )
        return carry

    lax.fori_loop(1, dp, greet, 0)

    ids = ids_ref[...]
    probs = probs_ref[...].astype(F32)
    lane = iota((8, rows), 0)
    spread = jnp.zeros((8, rows), F32)
    for k in range(ids.shape[0]):
        spread += jnp.where(lane == ids[k : k + 1, :], probs[k : k + 1, :], 0.0)
    meta[0] = spread

    slab[...] = jnp.zeros_like(slab)
    slab[0:nq, :] = unit_rows(tq_ref[0].astype(F32))[0]
    slab[nq : nq + npas, :] = unit_rows(tp_ref[0].astype(F32))[0]
    lane_row = iota((1, LANES), 1)
    pos_row = jnp.zeros((1, LANES), F32)
    for q in range(nq):
        value = pos_ref[0:1, q : q + 1]
        pos_row += jnp.where(lane_row == 2 * q, (value >> 6).astype(F32), 0.0)
        pos_row += jnp.where(lane_row == 2 * q + 1, (value & 63).astype(F32), 0.0)
    slab[nq + npas : nq + npas + 1, 0:LANES] = pos_row
    tmine[...] = slab[...].astype(BF16)

    pl.semaphore_wait(barrier, ex - 1 + dp - 1)

    token_copies = []
    for k in range(tok_chunks):
        at = pl.ds(k * chunk_rows, chunk_rows)
        to = pl.ds(far(2, k), chunk_rows)
        token_copies.append(remote(tok_ref.at[at], xbuf.at[to], cross))
    sib_copy = remote(tok_ref, xbuf.at[pl.ds(rows, rows)], sib)
    meta_copies = [remote(meta.at[0], meta.at[s], peers[s]) for s in range(1, ex)]
    token_copies[0].start()
    sib_copy.start()
    for copy in meta_copies:
        copy.start()
    for copy in token_copies[1:]:
        copy.start()

    def spread_copy(off, src, gath, s_sem, r_sem, incoming):
        slot = lax.rem(me + dp - off, dp) if incoming else me
        return pltpu.make_async_remote_copy(
            src_ref=src, dst_ref=gath.at[slot], send_sem=s_sem.at[off], recv_sem=r_sem.at[off],
            device_id=(lax.rem(me + off, dp), my_e), device_id_type=MESH,
        )

    def spread_start(src, gath, s_sem, r_sem):
        def body(off, carry):
            spread_copy(off, src, gath, s_sem, r_sem, False).start()
            return carry

        lax.fori_loop(1, dp, body, 0)
        gath[me] = src[...]

    def spread_wait(src, gath, s_sem, r_sem):
        def body(off, carry):
            spread_copy(off, src, gath, s_sem, r_sem, True).wait_recv()
            return carry

        lax.fori_loop(1, dp, body, 0)

    def spread_done(src, gath, s_sem, r_sem):
        def body(off, carry):
            spread_copy(off, src, gath, s_sem, r_sem, False).wait_send()
            return carry

        lax.fori_loop(1, dp, body, 0)

    spread_start(tmine, tgath, t_send, t_recv)

    tile = 256 if ff % 256 == 0 else ff

    def forward(start, count):
        at = pl.ds(start, count)

        def body(i, carry):
            cols = pl.ds(pl.multiple_of(i * tile, tile), tile)
            values = xbuf[at, :]
            gate = mm(values, wg[:, cols])
            up = mm(values, wu[:, cols])
            sig = 1.0 / (1.0 + jnp.exp(-gate))
            act = gate * sig
            hid[at, cols] = (act * up).astype(BF16)
            c2[at, cols] = act
            c1[at, cols] = up * (sig * (1.0 + gate * (1.0 - sig)))
            return carry

        lax.fori_loop(0, ff // tile, body, 0)

    loads[0].wait()
    loads[1].wait()
    loads[2].wait()
    sib_copy.wait_recv()
    forward(0, 2 * rows)
    forward_copies = []
    for k in range(tok_chunks):
        token_copies[k].wait_recv()
        copy = remote(
            xbuf.at[pl.ds(far(2, k), chunk_rows)], xbuf.at[pl.ds(far(3, k), chunk_rows)], sib
        )
        copy.start()
        forward_copies.append(copy)
        if k == tok_chunks // 2 - 1:
            for copy in forward_copies:
                copy.wait_recv()
            forward(2 * rows, rows)

    for copy in meta_copies:
        copy.wait_recv()
    t_at = iota((rp, rows), 1)
    segment = jnp.where(t_at < nq * QLEN, t_at // QLEN, nq + (t_at - nq * QLEN) // PLEN)
    member = segment == iota((rp, rows), 0)
    wf[...] = jnp.zeros_like(wf)
    for s in range(ex):
        prow = jnp.sum(jnp.where(iota((8, rows), 0) == my_e, meta[s], 0.0), axis=0, keepdims=True)
        weights = jnp.where(member, prow, 0.0)
        for start, count, token in places[s]:
            wf[s * rp : (s + 1) * rp, start : start + count] = weights[:, token : token + count]
    for s in range(ex):
        wt[s * rows : (s + 1) * rows, :] = jnp.transpose(wf[:, s * rows : (s + 1) * rows])
    loads[3].wait()

    for copy in forward_copies[tok_chunks // 2 :]:
        copy.wait_recv()
    forward(3 * rows, rows)

    nseg = ex * rp
    pooled_hid = mm(wf[0:nseg, :].astype(BF16), hid[...])
    high = pooled_hid.astype(BF16)
    low = (pooled_hid - high.astype(F32)).astype(BF16)
    both = jnp.concatenate([high, low], axis=0)

    def pooled_cols(j, carry):
        cols = pl.ds(pl.multiple_of(j * dc, dc), dc)
        part = mm(both, wd[:, cols])
        part = part[0:nseg] + part[nseg:]
        for s in range(ex):
            cbuf[s, :, cols] = part[s * rp : (s + 1) * rp, :].astype(BF16)
        return carry

    lax.fori_loop(0, col_chunks, pooled_cols, 0)
    pooled_copies = [remote(cbuf.at[s], crecv.at[s], peers[s]) for s in range(1, ex)]
    for s in (2, 3, 1):
        pooled_copies[s - 1].start()

    pcol = jnp.sum(wt[...], axis=1, keepdims=True)

    moe_a = [remote(s_a.at[0, j], r_a.at[0, j], sib) for j in range(col_chunks)]
    moe_b = [remote(s_b.at[0, j], r_b.at[0, j], cross) for j in range(col_chunks)]
    moe_c = remote(s_c.at[0], r_c.at[0], sib)

    def moe_part(j):
        part = mm(hid[...], wd[:, j * dc : (j + 1) * dc]) * pcol
        keep0[0, j] = part[0:rows]
        s_c[0, j] = part[rows : 2 * rows].astype(BF16)
        for start, count, token in places[2]:
            keep2[j, token : token + count] = part[start : start + count]
        for start, count, token in places[3]:
            s_a[0, j, token : token + count] = part[start : start + count].astype(BF16)
        moe_a[j].start()

    def moe_combine(j):
        moe_a[j].wait_recv()
        s_b[0, j] = (keep2[j] + r_a[0, j].astype(F32)).astype(BF16)

    early = col_chunks // 2
    for j in range(early):
        moe_part(j)

    for copy in pooled_copies:
        copy.wait_recv()
    row_at = iota((rp, 1), 0)
    is_query = row_at < nq
    total = cbuf[0].astype(F32)
    for s in range(1, ex):
        total += crecv[s].astype(F32)
    pooled = total * jnp.where(is_query, 1.0 / QLEN, 1.0 / PLEN)
    units, inverse = unit_rows(pooled)
    unit_buf[...] = units
    smine[...] = units.astype(BF16)
    spread_start(smine, sgath, s_send, s_recv)

    for j in range(early):
        moe_combine(j)
        moe_b[j].start()
    for j in range(early, col_chunks):
        moe_part(j)
    moe_c.start()
    for j in range(early, col_chunks):
        moe_combine(j)

    spread_wait(tmine, tgath, t_send, t_recv)
    for i in range(dp):
        tmat[i * rp : (i + 1) * rp, :] = tgath[i].astype(F32)
    tall = tmat[...].astype(BF16)
    teacher = teacher_scale * mm_last(tall, tall)
    n = dp * rp
    row = iota((n, n), 0)
    col = iota((n, n), 1)
    col_in = col % rp
    is_row = (row % rp) < nq
    is_pass = jnp.logical_and(col_in >= nq, col_in < nq + npas)
    live = jnp.logical_and(is_row, is_pass)
    pad_row = jnp.where(col == (row // rp) * rp + nq + npas, 1.0, 0.0).astype(BF16)
    codes = mm(pad_row, tall[:, 0:LANES])
    code_lane = iota((n, LANES), 1)
    code_at = 2 * (iota((n, LANES), 0) % rp)
    positive = jnp.sum(
        jnp.where(code_lane == code_at, codes * 64.0, 0.0)
        + jnp.where(code_lane == code_at + 1, codes, 0.0),
        axis=1,
        keepdims=True,
    ).astype(jnp.int32)
    is_pos = jnp.logical_and(live, ((col // rp) * npas + col_in - nq) == positive)
    teacher = jnp.where(live, teacher, 0.0)
    teacher_exp = jnp.where(live, jnp.exp(teacher), 0.0)
    teacher_total = jnp.sum(teacher_exp, axis=1, keepdims=True)
    row_live = (iota((n, 1), 0) % rp) < nq
    teacher_total = jnp.where(row_live, teacher_total, 1.0)

    spread_wait(smine, sgath, s_send, s_recv)
    for i in range(dp):
        smat[i * rp : (i + 1) * rp, :] = sgath[i].astype(F32)
    sall = smat[...].astype(BF16)
    student = jnp.where(live, student_scale * mm_last(sall, sall), 0.0)
    student_exp = jnp.where(live, jnp.exp(student), 0.0)
    student_total = jnp.where(row_live, jnp.sum(student_exp, axis=1, keepdims=True), 1.0)
    crossed = jnp.sum(teacher_exp * (teacher - student), axis=1, keepdims=True)
    pos_score = jnp.sum(jnp.where(is_pos, student, 0.0), axis=1, keepdims=True)
    loss = (
        2.0 * jnp.log(student_total) - pos_score + crossed / teacher_total - jnp.log(teacher_total)
    )
    coeffs = (
        2.0 * student_exp / student_total
        - teacher_exp / teacher_total
        - jnp.where(is_pos, 1.0, 0.0)
    ).astype(BF16)
    pick = jnp.where(iota((8, n), 1) == me * rp + iota((8, n), 0), 1.0, 0.0)
    pick = jnp.where(iota((8, n), 0) < rp, pick, 0.0).astype(BF16)
    mine = mm(pick, coeffs) + mm_last(pick, coeffs)
    unit_grad = (student_scale * mm(mine.astype(BF16), sall))[0:rp]
    for q in range(nq):
        chosen = jnp.where(iota((n, 1), 0) == me * rp + q, loss, 0.0)
        loss_ref[0:1, q : q + 1] = jnp.sum(chosen, axis=0, keepdims=True)
    units = unit_buf[...]
    grad = inverse * (unit_grad - units * jnp.sum(units * unit_grad, axis=-1, keepdims=True))
    grad = grad * jnp.where(is_query, loss_scale / QLEN, loss_scale / PLEN)
    ogmine[...] = grad.astype(BF16)
    og_copies = [remote(ogmine, ogbuf.at[s], peers[s]) for s in range(1, ex)]
    for s in (2, 3, 1):
        og_copies[s - 1].start()
    for copy in moe_b[early:]:
        copy.start()

    hgpad[...] = jnp.zeros_like(hgpad)
    ogmat[0:rp, :] = grad
    for s in (1, 3, 2):
        og_copies[s - 1].wait_recv()
    for s in range(1, ex):
        ogmat[s * rp : (s + 1) * rp, :] = ogbuf[s].astype(F32)
    hg = mm_last(ogmat[...].astype(BF16), wd[...]).astype(BF16)
    hgpad[0:nseg, :] = hg
    gpart = c1
    upart = c2

    def back_rows(start, count):
        at = pl.ds(start, count)
        hidden_grad = mm(wt[at, :].astype(BF16), hgpad[...])
        gate_part = (hidden_grad * gpart[at, :]).astype(BF16)
        up_part = (hidden_grad * upart[at, :]).astype(BF16)
        return gate_part, up_part

    tg_a = [remote(s_a.at[1, j], r_a.at[1, j], sib) for j in range(col_chunks)]
    tg_b = [remote(s_b.at[1, j], r_b.at[1, j], cross) for j in range(col_chunks)]
    tg_c = [remote(s_c.at[1, j], r_c.at[1, j], sib) for j in range(col_chunks)]

    def combine(j):
        tg_a[j].wait_recv()
        s_b[1, j] = (keep2[j] + r_a[1, j].astype(F32)).astype(BF16)
        tg_b[j].start()

    gate_part, up_part = back_rows(2 * rows, 2 * rows)
    for j in range(col_chunks):
        at = pl.ds(j * dc, dc)
        part = mm_last(gate_part, wg[at, :]) + mm_last(up_part, wu[at, :])
        for start, count, token in places[2]:
            keep2[j, token : token + count] = part[start - 2 * rows : start - 2 * rows + count]
        for start, count, token in places[3]:
            shifted = part[start - 2 * rows : start - 2 * rows + count]
            s_a[1, j, token : token + count] = shifted.astype(BF16)
        tg_a[j].start()
        if j:
            combine(j - 1)
    combine(col_chunks - 1)

    scores = mm_last(hg, hid[...])
    gg_copies = [remote(ggsend.at[s], ggrecv.at[s], peers[s]) for s in range(1, ex)]
    for s in range(ex):
        part = jnp.concatenate(
            [scores[s * rp : (s + 1) * rp, start : start + count] for start, count, _ in places[s]],
            axis=1,
        )
        line = jnp.sum(jnp.where(member, part, 0.0), axis=0, keepdims=True)
        ggsend[s] = jnp.where(iota((8, rows), 0) == my_e, line, 0.0)
    for copy in gg_copies:
        copy.start()

    gate_part, up_part = back_rows(0, 2 * rows)
    for j in range(col_chunks):
        at = pl.ds(j * dc, dc)
        part = mm_last(gate_part, wg[at, :]) + mm_last(up_part, wu[at, :])
        keep0[1, j] = part[0:rows]
        s_c[1, j] = part[rows:].astype(BF16)
        tg_c[j].start()

    writes = []

    def write(which, j, target):
        cols = pl.ds(j * dc, dc)
        copy = pltpu.make_async_copy(
            out_v.at[which, :, cols], target.at[:, cols], out_sem.at[which, j]
        )
        copy.start()
        writes.append(copy)

    moe_c.wait_recv()
    for j in range(col_chunks):
        moe_b[j].wait_recv()
        total = keep0[0, j] + r_c[0, j].astype(F32) + r_b[0, j].astype(F32)
        out_v[0, :, j * dc : (j + 1) * dc] = total.astype(BF16)
        write(0, j, moe_ref)
    for copy in gg_copies:
        copy.wait_recv()
    table = ggsend[0] + ggrecv[1] + ggrecv[2] + ggrecv[3]
    ids = ids_ref[...]
    for k in range(ids.shape[0]):
        chosen = jnp.where(lane == ids[k : k + 1, :], table, 0.0)
        ggrad_ref[k : k + 1, :] = jnp.sum(chosen, axis=0, keepdims=True)
    for j in range(col_chunks):
        tg_c[j].wait_recv()
        tg_b[j].wait_recv()
        total = keep0[1, j] + r_c[1, j].astype(F32) + r_b[1, j].astype(F32)
        out_v[1, :, j * dc : (j + 1) * dc] = total.astype(BF16)
        write(1, j, tgrad_ref)

    for copy in started:
        copy.wait_send()
    for copy in writes:
        copy.wait()
    spread_done(tmine, tgath, t_send, t_recv)
    spread_done(smine, sgath, s_send, s_recv)


def hand_on(moe_in, tgrad_in, ggrad_in, loss_in, moe, tgrad, ggrad, loss, held, in_sem, out_sem):
    chunks = in_sem.shape[1]
    count = moe_in.shape[0] // chunks
    loads, stores = [], []
    for k in range(chunks):
        at = pl.ds(k * count, count)
        for which, (src, dst) in enumerate(((moe_in, moe), (tgrad_in, tgrad))):
            slot = held.at[which, at]
            loads.append(pltpu.make_async_copy(src.at[at], slot, in_sem.at[which, k]))
            stores.append(pltpu.make_async_copy(slot, dst.at[at], out_sem.at[which, k]))
    for load in loads:
        load.start()
    ggrad[...] = ggrad_in[...]
    loss[...] = loss_in[...]
    for load, store in zip(loads, stores):
        load.wait()
        store.start()
    for store in stores:
        store.wait()


def shards(
    dp, ex,
    tokens, expert_ids, gate_probs, w_gate, w_up, w_down, teacher_queries, teacher_passages, positives,
):
    rows, width = tokens.shape
    ff = w_gate.shape[2]
    nq = teacher_queries.shape[1]
    npas = teacher_passages.shape[1]
    rp = -(-(nq + npas + 1) // 4) * 4
    tok_chunks, col_chunks = 4, 4
    dc = width // col_chunks
    dims = (dp, ex, rows, width, ff, nq, npas, rp, tok_chunks, col_chunks)
    copies = 2 * tok_chunks + 1 + 4 * (ex - 1) + 1 + 2 * col_chunks + 3 * col_chunks
    vmem = pl.BlockSpec(memory_space=pltpu.VMEM)
    hbm = pl.BlockSpec(memory_space=pl.ANY)
    dma = pltpu.SemaphoreType.DMA
    moved = pltpu.VMEM((2, col_chunks, rows, dc), BF16)
    moe, tgrad, ggrad, loss = pl.pallas_call(
        functools.partial(kernel, dims),
        out_shape=(
            jax.ShapeDtypeStruct((rows, width), BF16),
            jax.ShapeDtypeStruct((rows, width), BF16),
            jax.ShapeDtypeStruct(expert_ids.shape[::-1], F32),
            jax.ShapeDtypeStruct((1, nq), F32),
        ),
        in_specs=[hbm] * 4 + [vmem] * 5,
        out_specs=(hbm, hbm, vmem, vmem),
        scratch_shapes=[
            pltpu.VMEM((ex * rows, width), BF16),
            pltpu.VMEM((width, ff), BF16),
            pltpu.VMEM((width, ff), BF16),
            pltpu.VMEM((ff, width), BF16),
            pltpu.VMEM((ex * rows, ff), F32),
            pltpu.VMEM((ex * rows, ff), F32),
            pltpu.VMEM((ex * rows, ff), BF16),
            pltpu.VMEM((ex, 8, rows), F32),
            pltpu.VMEM((LANES, ex * rows), F32),
            pltpu.VMEM((ex * rows, LANES), F32),
            pltpu.VMEM((ex, rp, width), BF16),
            pltpu.VMEM((ex, rp, width), BF16),
            pltpu.VMEM((rp, width), F32),
            pltpu.VMEM((rp, width), BF16),
            pltpu.VMEM((rp, width), BF16),
            pltpu.VMEM((dp, rp, width), BF16),
            pltpu.VMEM((dp, rp, width), BF16),
            pltpu.VMEM((dp * rp, width), F32),
            pltpu.VMEM((dp * rp, width), F32),
            pltpu.VMEM((rp, width), F32),
            pltpu.VMEM((rp, width), BF16),
            pltpu.VMEM((ex, rp, width), BF16),
            pltpu.VMEM((ex * rp, width), F32),
            pltpu.VMEM((LANES, ff), BF16),
            pltpu.VMEM((ex, 8, rows), F32),
            pltpu.VMEM((ex, 8, rows), F32),
            moved, moved, moved, moved, moved, moved,
            pltpu.VMEM((2, col_chunks, rows, dc), F32),
            pltpu.VMEM((col_chunks, rows, dc), F32),
            pltpu.VMEM((2, rows, width), BF16),
            dma((copies,)), dma((copies,)),
            dma((dp,)), dma((dp,)), dma((dp,)), dma((dp,)),
            dma((4,)), dma((2, col_chunks)),
        ],
        compiler_params=pltpu.CompilerParams(
            collective_id=0, has_side_effects=True, vmem_limit_bytes=60 * 1024 * 1024
        ),
    )(
        tokens, w_gate, w_up, w_down, expert_ids.T, gate_probs.T,
        teacher_queries, teacher_passages, positives,
    )
    moe, tgrad, ggrad, loss = pl.pallas_call(
        hand_on,
        out_shape=tuple(jax.ShapeDtypeStruct(a.shape, a.dtype) for a in (moe, tgrad, ggrad, loss)),
        in_specs=[hbm, hbm, vmem, vmem],
        out_specs=(hbm, hbm, vmem, vmem),
        scratch_shapes=[pltpu.VMEM((2, rows, width), BF16), dma((2, 4)), dma((2, 4))],
        compiler_params=pltpu.CompilerParams(vmem_limit_bytes=60 * 1024 * 1024),
    )(moe, tgrad, ggrad, loss)
    return moe, tgrad, ggrad.T, loss


def solution(mesh):
    in_specs = (
        P(("dp", "expert"), None),
        P(("dp", "expert"), None),
        P(("dp", "expert"), None),
        P("expert", None, None),
        P("expert", None, None),
        P("expert", None, None),
        P("expert", "dp", None),
        P("expert", "dp", None),
        P("expert", "dp"),
    )
    out_specs = (
        P(("dp", "expert"), None),
        P(("dp", "expert"), None),
        P(("dp", "expert"), None),
        P("expert", "dp"),
    )
    body = functools.partial(shards, mesh.shape["dp"], mesh.shape["expert"])
    return jax.shard_map(body, mesh=mesh, in_specs=in_specs, out_specs=out_specs, check_vma=False)
```

```python
import functools

import jax
import jax.numpy as jnp
from jax import lax
from jax.experimental import pallas as pl
from jax.experimental.pallas import tpu as pltpu
from jax.sharding import PartitionSpec as P

QLEN = 32
PLEN = 48
student_scale = 50.0
teacher_scale = 80.0
loss_scale = 64.0
norm_eps = 1e-06
MESH = pl.DeviceIdType.MESH
F32 = jnp.float32
BF16 = jnp.bfloat16
LANES = 128


def mm(left, right):
    return jnp.dot(left, right, preferred_element_type=F32)


def mm_last(left, right):
    return lax.dot_general(left, right, (((1,), (1,)), ((), ())), preferred_element_type=F32)


def iota(shape, dim):
    return lax.broadcasted_iota(jnp.int32, shape, dim)


def unit_rows(values):
    inverse = lax.rsqrt(jnp.sum(values * values, axis=-1, keepdims=True) + norm_eps)
    return values * inverse, inverse


def kernel(
    dims,
    tok_ref, wg_hbm, wu_hbm, wd_hbm, ids_ref, probs_ref, tq_ref, tp_ref, pos_ref,
    moe_ref, tgrad_ref, ggrad_ref, loss_ref,
    xbuf, wg, wu, wd, c1, c2, hid, meta, wf, wt,
    cbuf, crecv, slab, tmine, smine, tgath, sgath, tmat, smat, unit_buf,
    ogmine, ogbuf, ogmat, hgpad, ggsend, ggrecv,
    s_a, r_a, s_b, r_b, s_c, r_c, keep0, keep2,
    out_v, send_sem, recv_sem, t_send, t_recv, s_send, s_recv, loc_sem, tok_sem, out_sem,
):
    dp, ex, rows, width, ff, nq, npas, rp, tok_chunks, col_chunks = dims
    me = lax.axis_index("dp")
    my_e = lax.axis_index("expert")
    half = ex // 2
    sib = my_e + 1 - 2 * lax.rem(my_e, 2)
    cross = lax.rem(my_e + half, ex)
    xsib = lax.rem(sib + half, ex)
    peers = [None, sib, cross, xsib]
    chunk_rows = rows // tok_chunks
    part_rows = rows // 2
    places = [
        [(0, rows, 0)],
        [(rows, rows, 0)],
        [(2 * rows, part_rows, 0), (3 * rows, part_rows, part_rows)],
        [(2 * rows + part_rows, part_rows, 0), (3 * rows + part_rows, part_rows, part_rows)],
    ]

    def far(slot, k):
        token = k * chunk_rows
        return 2 * rows + (token // part_rows) * rows + (slot - 2) * part_rows + token % part_rows

    dc = width // col_chunks
    counter = [0]
    started = []

    def remote(src, dst, target):
        at = counter[0]
        counter[0] += 1
        copy = pltpu.make_async_remote_copy(
            src_ref=src, dst_ref=dst, send_sem=send_sem.at[at], recv_sem=recv_sem.at[at],
            device_id=(me, target), device_id_type=MESH,
        )
        started.append(copy)
        return copy

    tok_load = pltpu.make_async_copy(tok_ref, xbuf.at[pl.ds(0, rows)], tok_sem)
    tok_load.start()
    weight_parts = loc_sem.shape[1]
    loads = []
    for which, (src, dst) in enumerate(((wg_hbm, wg), (wu_hbm, wu), (wd_hbm, wd))):
        count = dst.shape[0] // weight_parts
        for k in range(weight_parts):
            at = pl.ds(k * count, count)
            load = pltpu.make_async_copy(src.at[0, at], dst.at[at], loc_sem.at[which, k])
            load.start()
            loads.append(load)

    barrier = pltpu.get_barrier_semaphore()
    for peer in peers[1:]:
        pl.semaphore_signal(barrier, inc=1, device_id=(me, peer), device_id_type=MESH)

    def greet(off, carry):
        pl.semaphore_signal(
            barrier, inc=1, device_id=(lax.rem(me + off, dp), my_e), device_id_type=MESH
        )
        return carry

    lax.fori_loop(1, dp, greet, 0)

    ids = ids_ref[...]
    probs = probs_ref[...].astype(F32)
    lane = iota((8, rows), 0)
    spread = jnp.zeros((8, rows), F32)
    for k in range(ids.shape[0]):
        spread += jnp.where(lane == ids[k : k + 1, :], probs[k : k + 1, :], 0.0)
    meta[0] = spread

    slab[...] = jnp.zeros_like(slab)
    slab[0:nq, :] = unit_rows(tq_ref[0].astype(F32))[0]
    slab[nq : nq + npas, :] = unit_rows(tp_ref[0].astype(F32))[0]
    lane_row = iota((1, LANES), 1)
    pos_row = jnp.zeros((1, LANES), F32)
    for q in range(nq):
        value = pos_ref[0:1, q : q + 1]
        pos_row += jnp.where(lane_row == 2 * q, (value >> 6).astype(F32), 0.0)
        pos_row += jnp.where(lane_row == 2 * q + 1, (value & 63).astype(F32), 0.0)
    slab[nq + npas : nq + npas + 1, 0:LANES] = pos_row
    tmine[...] = slab[...].astype(BF16)

    pl.semaphore_wait(barrier, ex - 1 + dp - 1)

    token_copies = []
    for k in range(tok_chunks):
        at = pl.ds(k * chunk_rows, chunk_rows)
        to = pl.ds(far(2, k), chunk_rows)
        token_copies.append(remote(tok_ref.at[at], xbuf.at[to], cross))
    sib_copy = remote(tok_ref, xbuf.at[pl.ds(rows, rows)], sib)
    meta_copies = [remote(meta.at[0], meta.at[s], peers[s]) for s in range(1, ex)]
    token_copies[0].start()
    sib_copy.start()
    for copy in meta_copies:
        copy.start()
    for copy in token_copies[1:]:
        copy.start()

    def spread_copy(off, src, gath, s_sem, r_sem, incoming):
        slot = lax.rem(me + dp - off, dp) if incoming else me
        return pltpu.make_async_remote_copy(
            src_ref=src, dst_ref=gath.at[slot], send_sem=s_sem.at[off], recv_sem=r_sem.at[off],
            device_id=(lax.rem(me + off, dp), my_e), device_id_type=MESH,
        )

    def spread_start(src, gath, s_sem, r_sem):
        def body(off, carry):
            spread_copy(off, src, gath, s_sem, r_sem, False).start()
            return carry

        lax.fori_loop(1, dp, body, 0)
        gath[me] = src[...]

    def spread_wait(src, gath, s_sem, r_sem):
        def body(off, carry):
            spread_copy(off, src, gath, s_sem, r_sem, True).wait_recv()
            return carry

        lax.fori_loop(1, dp, body, 0)

    def spread_done(src, gath, s_sem, r_sem):
        def body(off, carry):
            spread_copy(off, src, gath, s_sem, r_sem, False).wait_send()
            return carry

        lax.fori_loop(1, dp, body, 0)

    spread_start(tmine, tgath, t_send, t_recv)

    tile = 256 if ff % 256 == 0 else ff

    def forward(start, count):
        at = pl.ds(start, count)

        def body(i, carry):
            cols = pl.ds(pl.multiple_of(i * tile, tile), tile)
            values = xbuf[at, :]
            gate = mm(values, wg[:, cols])
            up = mm(values, wu[:, cols])
            sig = 1.0 / (1.0 + jnp.exp(-gate))
            act = gate * sig
            hid[at, cols] = (act * up).astype(BF16)
            c2[at, cols] = act
            c1[at, cols] = up * (sig * (1.0 + gate * (1.0 - sig)))
            return carry

        lax.fori_loop(0, ff // tile, body, 0)

    tok_load.wait()
    for load in loads[: 2 * weight_parts]:
        load.wait()
    sib_copy.wait_recv()
    forward(0, 2 * rows)
    forward_copies = []
    for k in range(tok_chunks):
        token_copies[k].wait_recv()
        copy = remote(
            xbuf.at[pl.ds(far(2, k), chunk_rows)], xbuf.at[pl.ds(far(3, k), chunk_rows)], sib
        )
        copy.start()
        forward_copies.append(copy)
        if k == tok_chunks // 2 - 1:
            for copy in forward_copies:
                copy.wait_recv()
            forward(2 * rows, rows)

    for copy in meta_copies:
        copy.wait_recv()
    t_at = iota((rp, rows), 1)
    segment = jnp.where(t_at < nq * QLEN, t_at // QLEN, nq + (t_at - nq * QLEN) // PLEN)
    member = segment == iota((rp, rows), 0)
    wf[...] = jnp.zeros_like(wf)
    for s in range(ex):
        prow = jnp.sum(jnp.where(iota((8, rows), 0) == my_e, meta[s], 0.0), axis=0, keepdims=True)
        weights = jnp.where(member, prow, 0.0)
        for start, count, token in places[s]:
            wf[s * rp : (s + 1) * rp, start : start + count] = weights[:, token : token + count]
    for s in range(ex):
        wt[s * rows : (s + 1) * rows, :] = jnp.transpose(wf[:, s * rows : (s + 1) * rows])
    for load in loads[2 * weight_parts :]:
        load.wait()

    for copy in forward_copies[tok_chunks // 2 :]:
        copy.wait_recv()
    forward(3 * rows, rows)

    nseg = ex * rp
    pooled_hid = mm(wf[0:nseg, :].astype(BF16), hid[...])
    high = pooled_hid.astype(BF16)
    low = (pooled_hid - high.astype(F32)).astype(BF16)
    both = jnp.concatenate([high, low], axis=0)

    def pooled_cols(j, carry):
        cols = pl.ds(pl.multiple_of(j * dc, dc), dc)
        part = mm(both, wd[:, cols])
        part = part[0:nseg] + part[nseg:]
        for s in range(ex):
            cbuf[s, :, cols] = part[s * rp : (s + 1) * rp, :].astype(BF16)
        return carry

    lax.fori_loop(0, col_chunks, pooled_cols, 0)
    pooled_copies = [remote(cbuf.at[s], crecv.at[s], peers[s]) for s in range(1, ex)]
    for s in (2, 3, 1):
        pooled_copies[s - 1].start()

    pcol = jnp.sum(wt[...], axis=1, keepdims=True)

    moe_a = [remote(s_a.at[0, j], r_a.at[0, j], sib) for j in range(col_chunks)]
    moe_b = [remote(s_b.at[0, j], r_b.at[0, j], cross) for j in range(col_chunks)]
    moe_c = remote(s_c.at[0], r_c.at[0], sib)

    def moe_part(j):
        part = mm(hid[...], wd[:, j * dc : (j + 1) * dc]) * pcol
        keep0[0, j] = part[0:rows]
        s_c[0, j] = part[rows : 2 * rows].astype(BF16)
        for start, count, token in places[2]:
            keep2[j, token : token + count] = part[start : start + count]
        for start, count, token in places[3]:
            s_a[0, j, token : token + count] = part[start : start + count].astype(BF16)
        moe_a[j].start()

    def moe_combine(j):
        moe_a[j].wait_recv()
        s_b[0, j] = (keep2[j] + r_a[0, j].astype(F32)).astype(BF16)

    early = (3 * col_chunks) // 8
    for j in range(early):
        moe_part(j)

    for copy in pooled_copies:
        copy.wait_recv()
    row_at = iota((rp, 1), 0)
    is_query = row_at < nq
    total = cbuf[0].astype(F32)
    for s in range(1, ex):
        total += crecv[s].astype(F32)
    pooled = total * jnp.where(is_query, 1.0 / QLEN, 1.0 / PLEN)
    units, inverse = unit_rows(pooled)
    unit_buf[...] = units
    smine[...] = units.astype(BF16)
    spread_start(smine, sgath, s_send, s_recv)

    for j in range(early):
        moe_combine(j)
        moe_b[j].start()
    for j in range(early, col_chunks):
        moe_part(j)
    moe_c.start()
    for j in range(early, col_chunks):
        moe_combine(j)

    spread_wait(tmine, tgath, t_send, t_recv)
    for i in range(dp):
        tmat[i * rp : (i + 1) * rp, :] = tgath[i].astype(F32)
    tall = tmat[...].astype(BF16)
    teacher = teacher_scale * mm_last(tall, tall)
    n = dp * rp
    row = iota((n, n), 0)
    col = iota((n, n), 1)
    col_in = col % rp
    is_row = (row % rp) < nq
    is_pass = jnp.logical_and(col_in >= nq, col_in < nq + npas)
    live = jnp.logical_and(is_row, is_pass)
    pad_row = jnp.where(col == (row // rp) * rp + nq + npas, 1.0, 0.0).astype(BF16)
    codes = mm(pad_row, tall[:, 0:LANES])
    code_lane = iota((n, LANES), 1)
    code_at = 2 * (iota((n, LANES), 0) % rp)
    positive = jnp.sum(
        jnp.where(code_lane == code_at, codes * 64.0, 0.0)
        + jnp.where(code_lane == code_at + 1, codes, 0.0),
        axis=1,
        keepdims=True,
    ).astype(jnp.int32)
    is_pos = jnp.logical_and(live, ((col // rp) * npas + col_in - nq) == positive)
    teacher = jnp.where(live, teacher, 0.0)
    teacher_exp = jnp.where(live, jnp.exp(teacher), 0.0)
    teacher_total = jnp.sum(teacher_exp, axis=1, keepdims=True)
    row_live = (iota((n, 1), 0) % rp) < nq
    teacher_total = jnp.where(row_live, teacher_total, 1.0)

    spread_wait(smine, sgath, s_send, s_recv)
    for i in range(dp):
        smat[i * rp : (i + 1) * rp, :] = sgath[i].astype(F32)
    sall = smat[...].astype(BF16)
    student = jnp.where(live, student_scale * mm_last(sall, sall), 0.0)
    student_exp = jnp.where(live, jnp.exp(student), 0.0)
    student_total = jnp.where(row_live, jnp.sum(student_exp, axis=1, keepdims=True), 1.0)
    crossed = jnp.sum(teacher_exp * (teacher - student), axis=1, keepdims=True)
    pos_score = jnp.sum(jnp.where(is_pos, student, 0.0), axis=1, keepdims=True)
    loss = (
        2.0 * jnp.log(student_total) - pos_score + crossed / teacher_total - jnp.log(teacher_total)
    )
    coeffs = (
        2.0 * student_exp / student_total
        - teacher_exp / teacher_total
        - jnp.where(is_pos, 1.0, 0.0)
    ).astype(BF16)
    pick = jnp.where(iota((8, n), 1) == me * rp + iota((8, n), 0), 1.0, 0.0)
    pick = jnp.where(iota((8, n), 0) < rp, pick, 0.0).astype(BF16)
    mine = mm(pick, coeffs) + mm_last(pick, coeffs)
    unit_grad = (student_scale * mm(mine.astype(BF16), sall))[0:rp]
    for q in range(nq):
        chosen = jnp.where(iota((n, 1), 0) == me * rp + q, loss, 0.0)
        loss_ref[0:1, q : q + 1] = jnp.sum(chosen, axis=0, keepdims=True)
    units = unit_buf[...]
    grad = inverse * (unit_grad - units * jnp.sum(units * unit_grad, axis=-1, keepdims=True))
    grad = grad * jnp.where(is_query, loss_scale / QLEN, loss_scale / PLEN)
    ogmine[...] = grad.astype(BF16)
    og_copies = [remote(ogmine, ogbuf.at[s], peers[s]) for s in range(1, ex)]
    for s in (2, 3, 1):
        og_copies[s - 1].start()
    for copy in moe_b[early:]:
        copy.start()

    hgpad[...] = jnp.zeros_like(hgpad)
    ogmat[0:rp, :] = grad
    for s in (1, 3, 2):
        og_copies[s - 1].wait_recv()
    for s in range(1, ex):
        ogmat[s * rp : (s + 1) * rp, :] = ogbuf[s].astype(F32)
    hg = mm_last(ogmat[...].astype(BF16), wd[...]).astype(BF16)
    hgpad[0:nseg, :] = hg
    gpart = c1
    upart = c2

    def back_rows(start, count):
        at = pl.ds(start, count)
        hidden_grad = mm(wt[at, :].astype(BF16), hgpad[...])
        gate_part = (hidden_grad * gpart[at, :]).astype(BF16)
        up_part = (hidden_grad * upart[at, :]).astype(BF16)
        return gate_part, up_part

    tg_a = [remote(s_a.at[1, j], r_a.at[1, j], sib) for j in range(col_chunks)]
    tg_b = [remote(s_b.at[1, j], r_b.at[1, j], cross) for j in range(col_chunks)]
    tg_c = [remote(s_c.at[1, j], r_c.at[1, j], sib) for j in range(col_chunks)]

    def combine(j):
        tg_a[j].wait_recv()
        s_b[1, j] = (keep2[j] + r_a[1, j].astype(F32)).astype(BF16)
        tg_b[j].start()

    lag = 3
    gate_part, up_part = back_rows(2 * rows, 2 * rows)
    for j in range(col_chunks):
        at = pl.ds(j * dc, dc)
        part = mm_last(gate_part, wg[at, :]) + mm_last(up_part, wu[at, :])
        for start, count, token in places[2]:
            keep2[j, token : token + count] = part[start - 2 * rows : start - 2 * rows + count]
        for start, count, token in places[3]:
            shifted = part[start - 2 * rows : start - 2 * rows + count]
            s_a[1, j, token : token + count] = shifted.astype(BF16)
        tg_a[j].start()
        if j >= lag:
            combine(j - lag)
    for j in range(col_chunks - lag, col_chunks):
        combine(j)

    scores = mm_last(hg, hid[...])
    gg_copies = [remote(ggsend.at[s], ggrecv.at[s], peers[s]) for s in range(1, ex)]
    for s in range(ex):
        part = jnp.concatenate(
            [scores[s * rp : (s + 1) * rp, start : start + count] for start, count, _ in places[s]],
            axis=1,
        )
        line = jnp.sum(jnp.where(member, part, 0.0), axis=0, keepdims=True)
        ggsend[s] = jnp.where(iota((8, rows), 0) == my_e, line, 0.0)
    for copy in gg_copies:
        copy.start()

    gate_part, up_part = back_rows(0, 2 * rows)
    for j in range(col_chunks):
        at = pl.ds(j * dc, dc)
        part = mm_last(gate_part, wg[at, :]) + mm_last(up_part, wu[at, :])
        keep0[1, j] = part[0:rows]
        s_c[1, j] = part[rows:].astype(BF16)
        tg_c[j].start()

    writes = []

    def write(which, j, target):
        cols = pl.ds(j * dc, dc)
        copy = pltpu.make_async_copy(
            out_v.at[which, :, cols], target.at[:, cols], out_sem.at[which, j]
        )
        copy.start()
        writes.append(copy)

    moe_c.wait_recv()
    for j in range(col_chunks):
        moe_b[j].wait_recv()
        total = keep0[0, j] + r_c[0, j].astype(F32) + r_b[0, j].astype(F32)
        out_v[0, :, j * dc : (j + 1) * dc] = total.astype(BF16)
        write(0, j, moe_ref)
    for copy in gg_copies:
        copy.wait_recv()
    table = ggsend[0] + ggrecv[1] + ggrecv[2] + ggrecv[3]
    ids = ids_ref[...]
    for k in range(ids.shape[0]):
        chosen = jnp.where(lane == ids[k : k + 1, :], table, 0.0)
        ggrad_ref[k : k + 1, :] = jnp.sum(chosen, axis=0, keepdims=True)
    for j in range(col_chunks):
        tg_c[j].wait_recv()
        tg_b[j].wait_recv()
        total = keep0[1, j] + r_c[1, j].astype(F32) + r_b[1, j].astype(F32)
        out_v[1, :, j * dc : (j + 1) * dc] = total.astype(BF16)
        write(1, j, tgrad_ref)

    for copy in started:
        copy.wait_send()
    for copy in writes:
        copy.wait()
    spread_done(tmine, tgath, t_send, t_recv)
    spread_done(smine, sgath, s_send, s_recv)


def hand_on(
    moe_in, tgrad_in, ggrad_in, loss_in, moe, tgrad, ggrad, loss,
    held, held_ggrad, held_loss, in_sem, out_sem, small_sem,
):
    chunks = in_sem.shape[1]
    count = moe_in.shape[0] // chunks
    loads, stores = [], []
    for k in range(chunks):
        at = pl.ds(k * count, count)
        for which, (src, dst) in enumerate(((moe_in, moe), (tgrad_in, tgrad))):
            slot = held.at[which, at]
            loads.append(pltpu.make_async_copy(src.at[at], slot, in_sem.at[which, k]))
            stores.append(pltpu.make_async_copy(slot, dst.at[at], out_sem.at[which, k]))
    for k, (src, slot, dst) in enumerate(
        ((ggrad_in, held_ggrad, ggrad), (loss_in, held_loss, loss))
    ):
        loads.append(pltpu.make_async_copy(src, slot, small_sem.at[0, k]))
        stores.append(pltpu.make_async_copy(slot, dst, small_sem.at[1, k]))
    for load in loads:
        load.start()
    for load, store in zip(loads, stores):
        load.wait()
        store.start()
    for store in stores:
        store.wait()


def shards(
    dp, ex,
    tokens, expert_ids, gate_probs, w_gate, w_up, w_down, teacher_queries, teacher_passages, positives,
):
    rows, width = tokens.shape
    ff = w_gate.shape[2]
    nq = teacher_queries.shape[1]
    npas = teacher_passages.shape[1]
    rp = -(-(nq + npas + 1) // 4) * 4
    tok_chunks, col_chunks = 4, 8
    dc = width // col_chunks
    dims = (dp, ex, rows, width, ff, nq, npas, rp, tok_chunks, col_chunks)
    copies = 2 * tok_chunks + 1 + 4 * (ex - 1) + 1 + 2 * col_chunks + 3 * col_chunks
    vmem = pl.BlockSpec(memory_space=pltpu.VMEM)
    hbm = pl.BlockSpec(memory_space=pl.ANY)
    dma = pltpu.SemaphoreType.DMA
    moved = pltpu.VMEM((2, col_chunks, rows, dc), BF16)
    moe, tgrad, ggrad, loss = pl.pallas_call(
        functools.partial(kernel, dims),
        out_shape=(
            jax.ShapeDtypeStruct((rows, width), BF16),
            jax.ShapeDtypeStruct((rows, width), BF16),
            jax.ShapeDtypeStruct(expert_ids.shape[::-1], F32),
            jax.ShapeDtypeStruct((1, nq), F32),
        ),
        in_specs=[hbm] * 4 + [vmem] * 5,
        out_specs=(hbm, hbm, vmem, vmem),
        scratch_shapes=[
            pltpu.VMEM((ex * rows, width), BF16),
            pltpu.VMEM((width, ff), BF16),
            pltpu.VMEM((width, ff), BF16),
            pltpu.VMEM((ff, width), BF16),
            pltpu.VMEM((ex * rows, ff), F32),
            pltpu.VMEM((ex * rows, ff), F32),
            pltpu.VMEM((ex * rows, ff), BF16),
            pltpu.VMEM((ex, 8, rows), F32),
            pltpu.VMEM((LANES, ex * rows), F32),
            pltpu.VMEM((ex * rows, LANES), F32),
            pltpu.VMEM((ex, rp, width), BF16),
            pltpu.VMEM((ex, rp, width), BF16),
            pltpu.VMEM((rp, width), F32),
            pltpu.VMEM((rp, width), BF16),
            pltpu.VMEM((rp, width), BF16),
            pltpu.VMEM((dp, rp, width), BF16),
            pltpu.VMEM((dp, rp, width), BF16),
            pltpu.VMEM((dp * rp, width), F32),
            pltpu.VMEM((dp * rp, width), F32),
            pltpu.VMEM((rp, width), F32),
            pltpu.VMEM((rp, width), BF16),
            pltpu.VMEM((ex, rp, width), BF16),
            pltpu.VMEM((ex * rp, width), F32),
            pltpu.VMEM((LANES, ff), BF16),
            pltpu.VMEM((ex, 8, rows), F32),
            pltpu.VMEM((ex, 8, rows), F32),
            moved, moved, moved, moved, moved, moved,
            pltpu.VMEM((2, col_chunks, rows, dc), F32),
            pltpu.VMEM((col_chunks, rows, dc), F32),
            pltpu.VMEM((2, rows, width), BF16),
            dma((copies,)), dma((copies,)),
            dma((dp,)), dma((dp,)), dma((dp,)), dma((dp,)),
            dma((3, 4)), dma, dma((2, col_chunks)),
        ],
        compiler_params=pltpu.CompilerParams(
            collective_id=0, has_side_effects=True, vmem_limit_bytes=60 * 1024 * 1024
        ),
    )(
        tokens, w_gate, w_up, w_down, expert_ids.T, gate_probs.T,
        teacher_queries, teacher_passages, positives,
    )
    moe, tgrad, ggrad, loss = pl.pallas_call(
        hand_on,
        out_shape=tuple(jax.ShapeDtypeStruct(a.shape, a.dtype) for a in (moe, tgrad, ggrad, loss)),
        in_specs=[hbm] * 4,
        out_specs=(hbm,) * 4,
        scratch_shapes=[
            pltpu.VMEM((2, rows, width), BF16),
            pltpu.VMEM(ggrad.shape, F32),
            pltpu.VMEM(loss.shape, F32),
            dma((2, 2)), dma((2, 2)), dma((2, 2)),
        ],
        compiler_params=pltpu.CompilerParams(vmem_limit_bytes=60 * 1024 * 1024),
    )(moe, tgrad, ggrad, loss)
    return moe, tgrad, ggrad.T, loss


def solution(mesh):
    in_specs = (
        P(("dp", "expert"), None),
        P(("dp", "expert"), None),
        P(("dp", "expert"), None),
        P("expert", None, None),
        P("expert", None, None),
        P("expert", None, None),
        P("expert", "dp", None),
        P("expert", "dp", None),
        P("expert", "dp"),
    )
    out_specs = (
        P(("dp", "expert"), None),
        P(("dp", "expert"), None),
        P(("dp", "expert"), None),
        P("expert", "dp"),
    )
    body = functools.partial(shards, mesh.shape["dp"], mesh.shape["expert"])
    return jax.shard_map(body, mesh=mesh, in_specs=in_specs, out_specs=out_specs, check_vma=False)
```

```python
import functools

import jax
import jax.numpy as jnp
from jax import lax
from jax.experimental import pallas as pl
from jax.experimental.pallas import tpu as pltpu
from jax.sharding import PartitionSpec as P

QLEN = 32
PLEN = 48
student_scale = 50.0
teacher_scale = 80.0
loss_scale = 64.0
norm_eps = 1e-06
MESH = pl.DeviceIdType.MESH
F32 = jnp.float32
BF16 = jnp.bfloat16
LANES = 128


def mm(left, right):
    return jnp.dot(left, right, preferred_element_type=F32)


def mm_last(left, right):
    return lax.dot_general(left, right, (((1,), (1,)), ((), ())), preferred_element_type=F32)


def iota(shape, dim):
    return lax.broadcasted_iota(jnp.int32, shape, dim)


def unit_rows(values):
    inverse = lax.rsqrt(jnp.sum(values * values, axis=-1, keepdims=True) + norm_eps)
    return values * inverse, inverse


def kernel(
    dims,
    tok_ref, wg_hbm, wu_hbm, wd_hbm, ids_ref, probs_ref, tq_ref, tp_ref, pos_ref,
    moe_ref, tgrad_ref, ggrad_ref, loss_ref,
    xbuf, wg, wu, wd, c1, c2, hid, meta, wf, wt,
    cbuf, crecv, slab, tmine, smine, tgath, sgath, tmat, smat, unit_buf,
    ogmine, ogbuf, ogmat, hgpad, ggsend, ggrecv,
    s_a, r_a, s_b, r_b, s_c, r_c, keep0, keep2,
    out_v, send_sem, recv_sem, t_send, t_recv, s_send, s_recv, loc_sem, tok_sem, out_sem,
):
    dp, ex, rows, width, ff, nq, npas, rp, tok_chunks, col_chunks = dims
    me = lax.axis_index("dp")
    my_e = lax.axis_index("expert")
    half = ex // 2
    sib = my_e + 1 - 2 * lax.rem(my_e, 2)
    cross = lax.rem(my_e + half, ex)
    xsib = lax.rem(sib + half, ex)
    peers = [None, sib, cross, xsib]
    chunk_rows = rows // tok_chunks
    part_rows = rows // 2
    places = [
        [(0, rows, 0)],
        [(rows, rows, 0)],
        [(2 * rows, part_rows, 0), (3 * rows, part_rows, part_rows)],
        [(2 * rows + part_rows, part_rows, 0), (3 * rows + part_rows, part_rows, part_rows)],
    ]

    def far(slot, k):
        token = k * chunk_rows
        return 2 * rows + (token // part_rows) * rows + (slot - 2) * part_rows + token % part_rows

    dc = width // col_chunks
    counter = [0]
    started = []

    def remote(src, dst, target):
        at = counter[0]
        counter[0] += 1
        copy = pltpu.make_async_remote_copy(
            src_ref=src, dst_ref=dst, send_sem=send_sem.at[at], recv_sem=recv_sem.at[at],
            device_id=(me, target), device_id_type=MESH,
        )
        started.append(copy)
        return copy

    barrier = pltpu.get_barrier_semaphore()
    for peer in peers[1:]:
        pl.semaphore_signal(barrier, inc=1, device_id=(me, peer), device_id_type=MESH)

    def greet(off, carry):
        pl.semaphore_signal(
            barrier, inc=1, device_id=(lax.rem(me + off, dp), my_e), device_id_type=MESH
        )
        return carry

    lax.fori_loop(1, dp, greet, 0)

    tok_load = pltpu.make_async_copy(tok_ref, xbuf.at[pl.ds(0, rows)], tok_sem)
    tok_load.start()
    weight_parts = loc_sem.shape[1]
    loads = []
    for which, (src, dst) in enumerate(((wg_hbm, wg), (wu_hbm, wu), (wd_hbm, wd))):
        count = dst.shape[0] // weight_parts
        for k in range(weight_parts):
            at = pl.ds(k * count, count)
            load = pltpu.make_async_copy(src.at[0, at], dst.at[at], loc_sem.at[which, k])
            load.start()
            loads.append(load)

    ids = ids_ref[...]
    probs = probs_ref[...].astype(F32)
    lane = iota((8, rows), 0)
    spread = jnp.zeros((8, rows), F32)
    for k in range(ids.shape[0]):
        spread += jnp.where(lane == ids[k : k + 1, :], probs[k : k + 1, :], 0.0)
    meta[0] = spread

    slab[...] = jnp.zeros_like(slab)
    slab[0:nq, :] = unit_rows(tq_ref[0].astype(F32))[0]
    slab[nq : nq + npas, :] = unit_rows(tp_ref[0].astype(F32))[0]
    lane_row = iota((1, LANES), 1)
    pos_row = jnp.zeros((1, LANES), F32)
    for q in range(nq):
        value = pos_ref[0:1, q : q + 1]
        pos_row += jnp.where(lane_row == 2 * q, (value >> 6).astype(F32), 0.0)
        pos_row += jnp.where(lane_row == 2 * q + 1, (value & 63).astype(F32), 0.0)
    slab[nq + npas : nq + npas + 1, 0:LANES] = pos_row
    tmine[...] = slab[...].astype(BF16)

    pl.semaphore_wait(barrier, ex - 1 + dp - 1)

    token_copies = []
    for k in range(tok_chunks):
        at = pl.ds(k * chunk_rows, chunk_rows)
        to = pl.ds(far(2, k), chunk_rows)
        token_copies.append(remote(tok_ref.at[at], xbuf.at[to], cross))
    sib_copy = remote(tok_ref, xbuf.at[pl.ds(rows, rows)], sib)
    meta_copies = [remote(meta.at[0], meta.at[s], peers[s]) for s in range(1, ex)]
    token_copies[0].start()
    sib_copy.start()
    for copy in meta_copies:
        copy.start()
    for copy in token_copies[1:]:
        copy.start()

    def spread_copy(off, src, gath, s_sem, r_sem, incoming):
        slot = lax.rem(me + dp - off, dp) if incoming else me
        return pltpu.make_async_remote_copy(
            src_ref=src, dst_ref=gath.at[slot], send_sem=s_sem.at[off], recv_sem=r_sem.at[off],
            device_id=(lax.rem(me + off, dp), my_e), device_id_type=MESH,
        )

    def spread_start(src, gath, s_sem, r_sem):
        def body(off, carry):
            spread_copy(off, src, gath, s_sem, r_sem, False).start()
            return carry

        lax.fori_loop(1, dp, body, 0)
        gath[me] = src[...]

    def spread_wait(src, gath, s_sem, r_sem):
        def body(off, carry):
            spread_copy(off, src, gath, s_sem, r_sem, True).wait_recv()
            return carry

        lax.fori_loop(1, dp, body, 0)

    def spread_done(src, gath, s_sem, r_sem):
        def body(off, carry):
            spread_copy(off, src, gath, s_sem, r_sem, False).wait_send()
            return carry

        lax.fori_loop(1, dp, body, 0)

    spread_start(tmine, tgath, t_send, t_recv)

    tile = 256 if ff % 256 == 0 else ff

    def forward(start, count):
        at = pl.ds(start, count)

        def body(i, carry):
            cols = pl.ds(pl.multiple_of(i * tile, tile), tile)
            values = xbuf[at, :]
            gate = mm(values, wg[:, cols])
            up = mm(values, wu[:, cols])
            sig = 1.0 / (1.0 + jnp.exp(-gate))
            act = gate * sig
            hid[at, cols] = (act * up).astype(BF16)
            c2[at, cols] = act
            c1[at, cols] = up * (sig * (1.0 + gate * (1.0 - sig)))
            return carry

        lax.fori_loop(0, ff // tile, body, 0)

    tok_load.wait()
    for load in loads[: 2 * weight_parts]:
        load.wait()
    sib_copy.wait_recv()
    forward(0, 2 * rows)
    forward_copies = []

    def hand_over(first, last):
        for k in range(first, last):
            token_copies[k].wait_recv()
            copy = remote(
                xbuf.at[pl.ds(far(2, k), chunk_rows)], xbuf.at[pl.ds(far(3, k), chunk_rows)], sib
            )
            copy.start()
            forward_copies.append(copy)

    hand_over(0, tok_chunks // 2)

    spread_wait(tmine, tgath, t_send, t_recv)
    for i in range(dp):
        tmat[i * rp : (i + 1) * rp, :] = tgath[i].astype(F32)
    tall = tmat[...].astype(BF16)
    teacher = teacher_scale * mm_last(tall, tall)
    n = dp * rp
    row = iota((n, n), 0)
    col = iota((n, n), 1)
    col_in = col % rp
    is_row = (row % rp) < nq
    is_pass = jnp.logical_and(col_in >= nq, col_in < nq + npas)
    live = jnp.logical_and(is_row, is_pass)
    pad_row = jnp.where(col == (row // rp) * rp + nq + npas, 1.0, 0.0).astype(BF16)
    codes = mm(pad_row, tall[:, 0:LANES])
    code_lane = iota((n, LANES), 1)
    code_at = 2 * (iota((n, LANES), 0) % rp)
    positive = jnp.sum(
        jnp.where(code_lane == code_at, codes * 64.0, 0.0)
        + jnp.where(code_lane == code_at + 1, codes, 0.0),
        axis=1,
        keepdims=True,
    ).astype(jnp.int32)
    is_pos = jnp.logical_and(live, ((col // rp) * npas + col_in - nq) == positive)
    teacher = jnp.where(live, teacher, 0.0)
    teacher_exp = jnp.where(live, jnp.exp(teacher), 0.0)
    teacher_total = jnp.sum(teacher_exp, axis=1, keepdims=True)
    row_live = (iota((n, 1), 0) % rp) < nq
    teacher_total = jnp.where(row_live, teacher_total, 1.0)

    for copy in forward_copies:
        copy.wait_recv()
    forward(2 * rows, rows)
    hand_over(tok_chunks // 2, tok_chunks)

    for copy in meta_copies:
        copy.wait_recv()
    t_at = iota((rp, rows), 1)
    segment = jnp.where(t_at < nq * QLEN, t_at // QLEN, nq + (t_at - nq * QLEN) // PLEN)
    member = segment == iota((rp, rows), 0)
    wf[...] = jnp.zeros_like(wf)
    for s in range(ex):
        prow = jnp.sum(jnp.where(iota((8, rows), 0) == my_e, meta[s], 0.0), axis=0, keepdims=True)
        weights = jnp.where(member, prow, 0.0)
        for start, count, token in places[s]:
            wf[s * rp : (s + 1) * rp, start : start + count] = weights[:, token : token + count]
    for s in range(ex):
        wt[s * rows : (s + 1) * rows, :] = jnp.transpose(wf[:, s * rows : (s + 1) * rows])
    for load in loads[2 * weight_parts :]:
        load.wait()

    for copy in forward_copies[tok_chunks // 2 :]:
        copy.wait_recv()
    forward(3 * rows, rows)

    nseg = ex * rp
    pooled_hid = mm(wf[0:nseg, :].astype(BF16), hid[...])
    high = pooled_hid.astype(BF16)
    low = (pooled_hid - high.astype(F32)).astype(BF16)
    both = jnp.concatenate([high, low], axis=0)

    def pooled_cols(j, carry):
        cols = pl.ds(pl.multiple_of(j * dc, dc), dc)
        part = mm(both, wd[:, cols])
        part = part[0:nseg] + part[nseg:]
        for s in range(ex):
            cbuf[s, :, cols] = part[s * rp : (s + 1) * rp, :].astype(BF16)
        return carry

    lax.fori_loop(0, col_chunks, pooled_cols, 0)
    pooled_copies = [remote(cbuf.at[s], crecv.at[s], peers[s]) for s in range(1, ex)]
    for s in (2, 3, 1):
        pooled_copies[s - 1].start()

    pcol = jnp.sum(wt[...], axis=1, keepdims=True)

    moe_a = [remote(s_a.at[0, j], r_a.at[0, j], sib) for j in range(col_chunks)]
    moe_b = [remote(s_b.at[0, j], r_b.at[0, j], cross) for j in range(col_chunks)]
    moe_c = remote(s_c.at[0], r_c.at[0], sib)

    def moe_part(j):
        part = mm(hid[...], wd[:, j * dc : (j + 1) * dc]) * pcol
        keep0[0, j] = part[0:rows]
        s_c[0, j] = part[rows : 2 * rows].astype(BF16)
        for start, count, token in places[2]:
            keep2[j, token : token + count] = part[start : start + count]
        for start, count, token in places[3]:
            s_a[0, j, token : token + count] = part[start : start + count].astype(BF16)
        moe_a[j].start()

    def moe_combine(j):
        moe_a[j].wait_recv()
        s_b[0, j] = (keep2[j] + r_a[0, j].astype(F32)).astype(BF16)

    early = col_chunks // 2
    for j in range(early):
        moe_part(j)

    for copy in pooled_copies:
        copy.wait_recv()
    row_at = iota((rp, 1), 0)
    is_query = row_at < nq
    total = cbuf[0].astype(F32)
    for s in range(1, ex):
        total += crecv[s].astype(F32)
    pooled = total * jnp.where(is_query, 1.0 / QLEN, 1.0 / PLEN)
    units, inverse = unit_rows(pooled)
    unit_buf[...] = units
    smine[...] = units.astype(BF16)
    spread_start(smine, sgath, s_send, s_recv)

    for j in range(early):
        moe_combine(j)
        moe_b[j].start()
    moe_part(early)

    spread_wait(smine, sgath, s_send, s_recv)
    for i in range(dp):
        smat[i * rp : (i + 1) * rp, :] = sgath[i].astype(F32)
    sall = smat[...].astype(BF16)
    student = jnp.where(live, student_scale * mm_last(sall, sall), 0.0)
    student_exp = jnp.where(live, jnp.exp(student), 0.0)
    student_total = jnp.where(row_live, jnp.sum(student_exp, axis=1, keepdims=True), 1.0)
    crossed = jnp.sum(teacher_exp * (teacher - student), axis=1, keepdims=True)
    pos_score = jnp.sum(jnp.where(is_pos, student, 0.0), axis=1, keepdims=True)
    loss = (
        2.0 * jnp.log(student_total) - pos_score + crossed / teacher_total - jnp.log(teacher_total)
    )
    coeffs = (
        2.0 * student_exp / student_total
        - teacher_exp / teacher_total
        - jnp.where(is_pos, 1.0, 0.0)
    ).astype(BF16)
    pick = jnp.where(iota((8, n), 1) == me * rp + iota((8, n), 0), 1.0, 0.0)
    pick = jnp.where(iota((8, n), 0) < rp, pick, 0.0).astype(BF16)
    mine = mm(pick, coeffs) + mm_last(pick, coeffs)
    unit_grad = (student_scale * mm(mine.astype(BF16), sall))[0:rp]
    for q in range(nq):
        chosen = jnp.where(iota((n, 1), 0) == me * rp + q, loss, 0.0)
        loss_ref[0:1, q : q + 1] = jnp.sum(chosen, axis=0, keepdims=True)
    units = unit_buf[...]
    grad = inverse * (unit_grad - units * jnp.sum(units * unit_grad, axis=-1, keepdims=True))
    grad = grad * jnp.where(is_query, loss_scale / QLEN, loss_scale / PLEN)
    ogmine[...] = grad.astype(BF16)
    og_copies = [remote(ogmine, ogbuf.at[s], peers[s]) for s in range(1, ex)]
    for s in (2, 3, 1):
        og_copies[s - 1].start()
    for j in range(early + 1, col_chunks):
        moe_part(j)
    moe_c.start()
    for j in range(early, col_chunks):
        moe_combine(j)
        moe_b[j].start()

    hgpad[...] = jnp.zeros_like(hgpad)
    ogmat[0:rp, :] = grad
    for s in (1, 3, 2):
        og_copies[s - 1].wait_recv()
    for s in range(1, ex):
        ogmat[s * rp : (s + 1) * rp, :] = ogbuf[s].astype(F32)
    hg = mm_last(ogmat[...].astype(BF16), wd[...]).astype(BF16)
    hgpad[0:nseg, :] = hg
    gpart = c1
    upart = c2

    def back_rows(start, count):
        at = pl.ds(start, count)
        hidden_grad = mm(wt[at, :].astype(BF16), hgpad[...])
        gate_part = (hidden_grad * gpart[at, :]).astype(BF16)
        up_part = (hidden_grad * upart[at, :]).astype(BF16)
        return gate_part, up_part

    tg_a = [remote(s_a.at[1, j], r_a.at[1, j], sib) for j in range(col_chunks)]
    tg_b = [remote(s_b.at[1, j], r_b.at[1, j], cross) for j in range(col_chunks)]
    tg_c = [remote(s_c.at[1, j], r_c.at[1, j], sib) for j in range(col_chunks)]

    def combine(j):
        tg_a[j].wait_recv()
        s_b[1, j] = (keep2[j] + r_a[1, j].astype(F32)).astype(BF16)
        tg_b[j].start()

    lag = 1
    gate_part, up_part = back_rows(2 * rows, 2 * rows)
    for j in range(col_chunks):
        at = pl.ds(j * dc, dc)
        part = mm_last(gate_part, wg[at, :]) + mm_last(up_part, wu[at, :])
        for start, count, token in places[2]:
            keep2[j, token : token + count] = part[start - 2 * rows : start - 2 * rows + count]
        for start, count, token in places[3]:
            shifted = part[start - 2 * rows : start - 2 * rows + count]
            s_a[1, j, token : token + count] = shifted.astype(BF16)
        tg_a[j].start()
        if j >= lag:
            combine(j - lag)
    for j in range(col_chunks - lag, col_chunks):
        combine(j)

    scores = mm_last(hg, hid[...])
    gg_copies = [remote(ggsend.at[s], ggrecv.at[s], peers[s]) for s in range(1, ex)]
    for s in range(ex):
        part = jnp.concatenate(
            [scores[s * rp : (s + 1) * rp, start : start + count] for start, count, _ in places[s]],
            axis=1,
        )
        line = jnp.sum(jnp.where(member, part, 0.0), axis=0, keepdims=True)
        ggsend[s] = jnp.where(iota((8, rows), 0) == my_e, line, 0.0)
    for copy in gg_copies:
        copy.start()

    gate_part, up_part = back_rows(0, 2 * rows)
    for j in range(col_chunks):
        at = pl.ds(j * dc, dc)
        part = mm_last(gate_part, wg[at, :]) + mm_last(up_part, wu[at, :])
        keep0[1, j] = part[0:rows]
        s_c[1, j] = part[rows:].astype(BF16)
        tg_c[j].start()

    writes = []

    def write(which, j, target):
        cols = pl.ds(j * dc, dc)
        copy = pltpu.make_async_copy(
            out_v.at[which, :, cols], target.at[:, cols], out_sem.at[which, j]
        )
        copy.start()
        writes.append(copy)

    moe_c.wait_recv()
    for j in range(col_chunks):
        moe_b[j].wait_recv()
        total = keep0[0, j] + r_c[0, j].astype(F32) + r_b[0, j].astype(F32)
        out_v[0, :, j * dc : (j + 1) * dc] = total.astype(BF16)
        write(0, j, moe_ref)
    for copy in gg_copies:
        copy.wait_recv()
    table = ggsend[0] + ggrecv[1] + ggrecv[2] + ggrecv[3]
    ids = ids_ref[...]
    for k in range(ids.shape[0]):
        chosen = jnp.where(lane == ids[k : k + 1, :], table, 0.0)
        ggrad_ref[k : k + 1, :] = jnp.sum(chosen, axis=0, keepdims=True)
    for j in range(col_chunks):
        tg_c[j].wait_recv()
        tg_b[j].wait_recv()
        total = keep0[1, j] + r_c[1, j].astype(F32) + r_b[1, j].astype(F32)
        out_v[1, :, j * dc : (j + 1) * dc] = total.astype(BF16)
        write(1, j, tgrad_ref)

    for copy in started:
        copy.wait_send()
    for copy in writes:
        copy.wait()
    spread_done(tmine, tgath, t_send, t_recv)
    spread_done(smine, sgath, s_send, s_recv)


def hand_on(
    moe_in, tgrad_in, ggrad_in, loss_in, moe, tgrad, ggrad, loss,
    held, held_ggrad, held_loss, in_sem, out_sem, small_sem,
):
    chunks = in_sem.shape[1]
    count = moe_in.shape[0] // chunks
    loads, stores = [], []
    for k in range(chunks):
        at = pl.ds(k * count, count)
        for which, (src, dst) in enumerate(((moe_in, moe), (tgrad_in, tgrad))):
            slot = held.at[which, at]
            loads.append(pltpu.make_async_copy(src.at[at], slot, in_sem.at[which, k]))
            stores.append(pltpu.make_async_copy(slot, dst.at[at], out_sem.at[which, k]))
    for k, (src, slot, dst) in enumerate(
        ((ggrad_in, held_ggrad, ggrad), (loss_in, held_loss, loss))
    ):
        loads.append(pltpu.make_async_copy(src, slot, small_sem.at[0, k]))
        stores.append(pltpu.make_async_copy(slot, dst, small_sem.at[1, k]))
    for load in loads:
        load.start()
    for load, store in zip(loads, stores):
        load.wait()
        store.start()
    for store in stores:
        store.wait()


def shards(
    dp, ex,
    tokens, expert_ids, gate_probs, w_gate, w_up, w_down, teacher_queries, teacher_passages, positives,
):
    rows, width = tokens.shape
    ff = w_gate.shape[2]
    nq = teacher_queries.shape[1]
    npas = teacher_passages.shape[1]
    rp = -(-(nq + npas + 1) // 4) * 4
    tok_chunks, col_chunks = 4, 4
    dc = width // col_chunks
    dims = (dp, ex, rows, width, ff, nq, npas, rp, tok_chunks, col_chunks)
    copies = 2 * tok_chunks + 1 + 4 * (ex - 1) + 1 + 2 * col_chunks + 3 * col_chunks
    vmem = pl.BlockSpec(memory_space=pltpu.VMEM)
    hbm = pl.BlockSpec(memory_space=pl.ANY)
    dma = pltpu.SemaphoreType.DMA
    moved = pltpu.VMEM((2, col_chunks, rows, dc), BF16)
    moe, tgrad, ggrad, loss = pl.pallas_call(
        functools.partial(kernel, dims),
        out_shape=(
            jax.ShapeDtypeStruct((rows, width), BF16),
            jax.ShapeDtypeStruct((rows, width), BF16),
            jax.ShapeDtypeStruct(expert_ids.shape[::-1], F32),
            jax.ShapeDtypeStruct((1, nq), F32),
        ),
        in_specs=[hbm] * 4 + [vmem] * 5,
        out_specs=(hbm, hbm, vmem, vmem),
        scratch_shapes=[
            pltpu.VMEM((ex * rows, width), BF16),
            pltpu.VMEM((width, ff), BF16),
            pltpu.VMEM((width, ff), BF16),
            pltpu.VMEM((ff, width), BF16),
            pltpu.VMEM((ex * rows, ff), F32),
            pltpu.VMEM((ex * rows, ff), F32),
            pltpu.VMEM((ex * rows, ff), BF16),
            pltpu.VMEM((ex, 8, rows), F32),
            pltpu.VMEM((LANES, ex * rows), F32),
            pltpu.VMEM((ex * rows, LANES), F32),
            pltpu.VMEM((ex, rp, width), BF16),
            pltpu.VMEM((ex, rp, width), BF16),
            pltpu.VMEM((rp, width), F32),
            pltpu.VMEM((rp, width), BF16),
            pltpu.VMEM((rp, width), BF16),
            pltpu.VMEM((dp, rp, width), BF16),
            pltpu.VMEM((dp, rp, width), BF16),
            pltpu.VMEM((dp * rp, width), F32),
            pltpu.VMEM((dp * rp, width), F32),
            pltpu.VMEM((rp, width), F32),
            pltpu.VMEM((rp, width), BF16),
            pltpu.VMEM((ex, rp, width), BF16),
            pltpu.VMEM((ex * rp, width), F32),
            pltpu.VMEM((LANES, ff), BF16),
            pltpu.VMEM((ex, 8, rows), F32),
            pltpu.VMEM((ex, 8, rows), F32),
            moved, moved, moved, moved, moved, moved,
            pltpu.VMEM((2, col_chunks, rows, dc), F32),
            pltpu.VMEM((col_chunks, rows, dc), F32),
            pltpu.VMEM((2, rows, width), BF16),
            dma((copies,)), dma((copies,)),
            dma((dp,)), dma((dp,)), dma((dp,)), dma((dp,)),
            dma((3, 1)), dma, dma((2, col_chunks)),
        ],
        compiler_params=pltpu.CompilerParams(
            collective_id=0, has_side_effects=True, vmem_limit_bytes=60 * 1024 * 1024
        ),
    )(
        tokens, w_gate, w_up, w_down, expert_ids.T, gate_probs.T,
        teacher_queries, teacher_passages, positives,
    )
    moe, tgrad, ggrad, loss = pl.pallas_call(
        hand_on,
        out_shape=tuple(jax.ShapeDtypeStruct(a.shape, a.dtype) for a in (moe, tgrad, ggrad, loss)),
        in_specs=[hbm] * 4,
        out_specs=(hbm,) * 4,
        scratch_shapes=[
            pltpu.VMEM((2, rows, width), BF16),
            pltpu.VMEM(ggrad.shape, F32),
            pltpu.VMEM(loss.shape, F32),
            dma((2, 2)), dma((2, 2)), dma((2, 2)),
        ],
        compiler_params=pltpu.CompilerParams(vmem_limit_bytes=60 * 1024 * 1024),
    )(moe, tgrad, ggrad, loss)
    return moe, tgrad, ggrad.T, loss


def solution(mesh):
    in_specs = (
        P(("dp", "expert"), None),
        P(("dp", "expert"), None),
        P(("dp", "expert"), None),
        P("expert", None, None),
        P("expert", None, None),
        P("expert", None, None),
        P("expert", "dp", None),
        P("expert", "dp", None),
        P("expert", "dp"),
    )
    out_specs = (
        P(("dp", "expert"), None),
        P(("dp", "expert"), None),
        P(("dp", "expert"), None),
        P("expert", "dp"),
    )
    body = functools.partial(shards, mesh.shape["dp"], mesh.shape["expert"])
    return jax.shard_map(body, mesh=mesh, in_specs=in_specs, out_specs=out_specs, check_vma=False)
```
